32 devices in a mesh: tm: 4 (over y, core), gx: 8 (over z, x).
Axes of the slice: x: 2, y: 2, z: 4, core: 2. Of those that a mesh axis runs over, the one named last changes fastest.
Arguments:
- end_modes: float32 [4, 256, 256, 256], P('tm', None, 'gx'), may hold values from -1 to 1
- initial_modes: float32 [256, 256, 256], P(None, 'gx'), may hold values from -1 to 1
Outputs:
- new_end_modes: float32 [4, 256, 256, 256], P('tm', None, 'gx')
- coarse_ends: float32 [4, 128, 128, 128], P('tm', None, 'gx')
The draws below stay inside these ranges and needn't reach their ends.
All inputs are finite; a program needn't handle non-finite values.
Results may differ from the reference program's by a relative error of at most 0.00014.
Values sent between devices are 32-bit elements; how exact they have to be, the bound alone decides.
No kernel may reach another device: no remote copies, remote signals or barrier semaphores. Data moves between devices by JAX's collectives and lax.ppermute only.
A program may use at most 192 MiB of HBM per device.

```python
import math
import jax
import jax.numpy as jnp

GRID = 256
SLICES = 4
N_GX = 8


def draw_end_modes(key, part):
    own_key = jax.random.fold_in(key, 11)
    extent = (SLICES, GRID, GRID, GRID)
    values = jnp.clip(0.25 * jax.random.normal(own_key, extent, jnp.float32), -1.0, 1.0)
    return values


def draw_initial_modes(key, part):
    own_key = jax.random.fold_in(key, 23)
    extent = (GRID, GRID, GRID)
    values = jnp.clip(0.25 * jax.random.normal(own_key, extent, jnp.float32), -1.0, 1.0)
    return values


def setup_inputs(seed: int = 0) -> dict:
    arg_keys = jax.random.split(jax.random.key(seed), 3)
    end_modes = draw_end_modes(jax.random.fold_in(arg_keys[2], 71), 0)
    initial_modes = draw_initial_modes(jax.random.fold_in(arg_keys[2], 71), 0)
    return dict(end_modes=end_modes, initial_modes=initial_modes)


DIFFUSION = 0.25

def sine_axis(field, axis):
    length = field.shape[axis]
    moved = jnp.moveaxis(field, axis, -1)
    zero = jnp.zeros(moved.shape[:-1] + (1,), moved.dtype)
    extended = jnp.concatenate([zero, moved, zero, -moved[..., ::-1]], axis=-1)
    spectrum = jnp.fft.rfft(extended, axis=-1)
    result = -jnp.imag(spectrum[..., 1:length + 1]) * (0.5 * math.sqrt(2.0 / (length + 1)))
    return jnp.moveaxis(result.astype(field.dtype), -1, axis)

def sine_cube(field):
    return sine_axis(sine_axis(sine_axis(field, 0), 1), 2)

def omega(count):
    modes = jnp.arange(count, dtype=jnp.int32).astype(jnp.float32)
    return 2.0 - 2.0 * jnp.cos((modes + 1.0) * (math.pi / (count + 1)))

def reaction(field):
    return field - field * field * field

def reference(end_modes, initial_modes):
    grid = GRID
    coarse = grid // 2
    block = grid // N_GX
    half = block // 2
    positions = jnp.arange(grid, dtype=jnp.int32)
    within = positions % block
    group = positions // block
    mode_of = jnp.where(within < half, group * half + within, coarse + group * half + within - half).astype(jnp.int32)
    lower = positions < coarse
    shifted = jnp.where(lower, positions, positions - coarse)
    position_of = (shifted // half * block + shifted % half + jnp.where(lower, 0, half)).astype(jnp.int32)
    fine_w = omega(grid)
    coarse_w = omega(coarse)
    fine_eigen = DIFFUSION * (fine_w[:, None, None] + fine_w[None, :, None] + fine_w[None, None, :])
    coarse_eigen = 0.25 * DIFFUSION * (coarse_w[:, None, None] + coarse_w[None, :, None] + coarse_w[None, None, :])
    factor = ((coarse + 1) / (grid + 1)) ** 1.5

    def natural(modes):
        return jnp.take(modes, position_of, axis=1)

    def restrict(modes):
        return factor * modes[:coarse, :coarse, :coarse]
    low_eigen = fine_eigen[:coarse, :coarse, :coarse]
    new_list = []
    coarse_list = []
    previous_coarse = None
    for slice_number in range(SLICES):
        if slice_number == 0:
            start_modes = natural(initial_modes)
        else:
            start_modes = natural(end_modes[slice_number - 1])
        start_field = sine_cube(start_modes)
        start_reaction = sine_cube(reaction(start_field))
        node_mid = (start_modes + 0.5 * start_reaction) / (1.0 + 0.5 * fine_eigen)
        node_end = (start_modes + start_reaction) / (1.0 + fine_eigen)
        mid_reaction = restrict(sine_cube(reaction(sine_cube(node_mid))))
        end_reaction = restrict(sine_cube(reaction(sine_cube(node_end))))
        first_term = restrict(start_reaction) - low_eigen * restrict(start_modes)
        mid_term = mid_reaction - low_eigen * restrict(node_mid)
        end_term = end_reaction - low_eigen * restrict(node_end)
        integral = (first_term + 4.0 * mid_term + end_term) / 6.0
        if slice_number == 0:
            coarse_start = restrict(start_modes)
        else:
            coarse_start = previous_coarse
        coarse_end = (coarse_start + integral + coarse_eigen * restrict(node_end)) / (1.0 + coarse_eigen)
        previous_coarse = coarse_end
        corrected = node_end.at[:coarse, :coarse, :coarse].set(coarse_end / factor)
        new_list.append(jnp.take(corrected, mode_of, axis=1))
        coarse_list.append(coarse_end)
    return (jnp.stack(new_list), jnp.stack(coarse_list))
```

```python
import functools
import math

import jax
import jax.numpy as jnp
import ml_dtypes
import numpy as np
from jax import lax
from jax.experimental import pallas as pl
from jax.experimental.pallas import tpu as pltpu
from jax.sharding import PartitionSpec as P

DIFFUSION = 0.25
BF16 = jnp.bfloat16
F32 = jnp.float32
ROWS = 8
VMEM_BYTES = 56 * 1024 * 1024


def sine_matrix(length):
    index = np.arange(1, length + 1)
    phase = np.outer(index, index) % (2 * (length + 1))
    return np.sin(phase * (math.pi / (length + 1))) * math.sqrt(2.0 / (length + 1))


def omega(count):
    return 2.0 - 2.0 * np.cos((np.arange(count) + 1.0) * (math.pi / (count + 1)))


def fine_order(grid, groups):
    block, coarse = grid // groups, grid // 2
    half = block // 2
    position = np.arange(grid)
    within, group = position % block, position // block
    return np.where(within < half, group * half + within, coarse + group * half + within - half)


def halves(table):
    high = table.astype(ml_dtypes.bfloat16)
    low = (table - high.astype(np.float64)).astype(ml_dtypes.bfloat16)
    return high, low


def left_table(table):
    high, low = halves(table)
    return np.concatenate([high, high, low], axis=1)


def right_table(table):
    high, low = halves(table)
    return np.concatenate([high, high, low], axis=0)


def split3(value, axis):
    high = value.astype(BF16)
    low = (value - high.astype(F32)).astype(BF16)
    return jnp.concatenate([high, low, high], axis=axis)


def left(table, value):
    return jnp.dot(table, split3(value, 0), preferred_element_type=F32)


def right(value, table):
    return jnp.dot(split3(value, 1), table, preferred_element_type=F32)


def cube(value):
    return value * value * value


def whole_block(shape):
    return pl.BlockSpec(shape, lambda *_: (0,) * len(shape))


SMEM = pl.BlockSpec(memory_space=pltpu.SMEM)


def call(kernel, name, grid, in_specs, out_specs, out_shape, scratch=(), flops=0, moved=0, aliases=None):
    return pl.pallas_call(
        kernel,
        grid=grid,
        in_specs=in_specs,
        out_specs=out_specs,
        out_shape=out_shape,
        scratch_shapes=list(scratch),
        input_output_aliases=aliases or {},
        compiler_params=pltpu.CompilerParams(vmem_limit_bytes=VMEM_BYTES),
        cost_estimate=pl.CostEstimate(flops=flops, bytes_accessed=moved, transcendentals=0),
        name=name,
    )


def depth_kernel(first_ref, table_ref, initial_ref, previous_ref, out_ref):
    first = first_ref[0] == 1
    for row in range(ROWS):
        value = jnp.where(first, initial_ref[:, row, :], previous_ref[:, row, :])
        out_ref[:, row, :] = left(table_ref[...], value)


def start_kernel(planes, modes_ref, sx_ref, sy_ref, syt_ref, rho_ref,
                 low_ref, high_ref, v_ref, to_right_ref, to_left_ref, power):
    step = pl.program_id(0)

    @pl.when(step == 0)
    def _():
        power[...] = jnp.ones_like(power)
        to_right_ref[...] = jnp.zeros_like(to_right_ref)
        to_left_ref[...] = jnp.zeros_like(to_left_ref)

    groups, _, block, wide = modes_ref.shape
    grid = groups * block
    half = block // 2
    modes = [modes_ref[:, j].reshape(grid, wide) for j in range(planes)]
    along_x = right(jnp.concatenate(modes, axis=0), sx_ref[...])
    terms = [cube(left(sy_ref[...], along_x[j * grid:(j + 1) * grid])) for j in range(planes)]
    along_x = right(jnp.concatenate(terms, axis=0), sx_ref[...])
    for j in reversed(range(planes)):
        cubic = left(syt_ref[...], along_x[j * grid:(j + 1) * grid])
        source_end = 2.0 * modes[j] - cubic
        parts = source_end.reshape(groups, block, wide)
        low_ref[:, j] = parts[:, :half]
        high_ref[:, j] = parts[:, half:]
        for node, source in enumerate((source_end, 0.5 * (modes[j] + source_end))):
            rho = rho_ref[node]
            carried = source + rho * to_left_ref[node]
            to_left_ref[node] = carried
            v_ref[node, j] = carried
            to_right_ref[node] += power[node] * source
            power[node] = power[node] * rho


def node_kernel(planes, slab, modes_ref, low_ref, high_ref, v_ref, from_left_ref, from_right_ref,
                rho_ref, inverse_ref, kappa_ref, sx_ref, sy_ref, sxl_ref, syl_ref,
                out_ref, left_sum, right_sum):
    step = pl.program_id(0)

    @pl.when(step == 0)
    def _():
        left_sum[...] = from_left_ref[...]

    @pl.when(step * planes % ROWS == 0)
    def _():
        rho = rho_ref[...]
        twice = rho * rho
        four = twice * twice
        eight = four * four
        right_sum[...] = lax.fori_loop(
            0, slab // ROWS - step * planes // ROWS, lambda _, total: total * eight, from_right_ref[...]
        )

    groups, _, block, wide = modes_ref.shape
    grid = groups * block
    nodes = []
    for j in range(planes):
        source_end = jnp.concatenate([low_ref[:, j], high_ref[:, j]], axis=1).reshape(grid, wide)
        source_mid = 0.5 * (modes_ref[:, j].reshape(grid, wide) + source_end)
        for node, source in enumerate((source_end, source_mid)):
            behind = rho_ref[node] * left_sum[node]
            left_sum[node] = source + behind
            nodes.append(kappa_ref[node] * (behind + v_ref[node, j] + right_sum[node]))
            right_sum[node] = right_sum[node] * inverse_ref[node]
    along_x = right(jnp.concatenate(nodes, axis=0), sx_ref[...])
    fields = [left(sy_ref[...], along_x[j * grid:(j + 1) * grid]) for j in range(2 * planes)]
    terms = [cube(fields[2 * j]) + 4.0 * cube(fields[2 * j + 1]) for j in range(planes)]
    along_x = right(jnp.concatenate(terms, axis=0), sxl_ref[...])
    for j in range(planes):
        term = left(syl_ref[...], along_x[j * grid:(j + 1) * grid])
        out_ref[:, j] = term.reshape(groups, block // 2, wide // 2)


def low_kernel(factor, fine_ref, coarse_ref, table_ref, eigen_ref, coarse_eigen_ref, source_ref, start_ref,
               out_ref, gathered_ref):
    base = pl.program_id(0) * ROWS
    coarse = start_ref.shape[0]
    for row in range(ROWS):
        source = left(table_ref[...], source_ref[:, row, :])
        eigen = eigen_ref[...] + fine_ref[base + row]
        node_end = source / (1.0 + eigen)
        out_ref[:, row, :] = node_end
        source, node_end, eigen = source[:coarse, :coarse], node_end[:coarse, :coarse], eigen[:coarse, :coarse]
        start = start_ref[:, row, :]
        node_mid = 0.5 * (start + source) / (1.0 + 0.5 * eigen)
        rate = source - (1.0 + eigen) * start + (1.0 - eigen) * (4.0 * node_mid + node_end)
        coarse_eigen = coarse_eigen_ref[...] + coarse_ref[base + row]
        gathered_ref[:, row, :] = factor * (rate / 6.0 + coarse_eigen * node_end)


def offset_kernel(factor, first_ref, coarse_ref, table_ref, coarse_eigen_ref, cubic_ref, gathered_ref, start_ref,
                  out_ref):
    base = pl.program_id(0) * ROWS
    first = first_ref[0] == 1
    for row in range(ROWS):
        cubic = left(table_ref[...], cubic_ref[:, row, :])
        total = gathered_ref[:, row, :] - (factor / 6.0) * cubic
        total += jnp.where(first, factor * start_ref[:, row, :], 0.0)
        out_ref[:, row, :] = total / (1.0 + coarse_eigen_ref[...] + coarse_ref[base + row])


def high_kernel(fine_ref, table_ref, eigen_ref, source_ref, _, out_ref):
    base = pl.program_id(0) * ROWS
    for row in range(ROWS):
        source = left(table_ref[...], source_ref[:, row, :])
        out_ref[:, row, :] = source / (1.0 + eigen_ref[...] + fine_ref[base + row])


def shifted(value, axis, by):
    length = lax.axis_size(axis)
    pairs = [(i, i + by) for i in range(length) if 0 <= i + by < length]
    return lax.ppermute(value, axis, pairs)


def exchange(value):
    return lax.all_to_all(value, "gx", split_axis=0, concat_axis=0, tiled=True)


def per_device(end_modes, initial_modes):
    grid = initial_modes.shape[0]
    coarse = grid // 2
    groups = lax.axis_size("gx")
    block = grid // groups
    half = block // 2
    planes = 2
    slice_index = lax.axis_index("tm")
    group_index = lax.axis_index("gx")
    is_first = slice_index == 0
    first = is_first.astype(jnp.int32)[None]
    order = fine_order(grid, groups)
    sine = sine_matrix(grid)
    fine_w, coarse_w = omega(grid), omega(coarse)
    factor = ((coarse + 1) / (grid + 1)) ** 1.5
    unit = grid * block * grid

    flat = fine_w[order][:, None] + fine_w[None, :]
    scale = np.array([1.0, 0.5])[:, None, None] * DIFFUSION
    diagonal = 1.0 / scale + 2.0 + flat[None]
    rho = 2.0 / (diagonal + np.sqrt(diagonal * diagonal - 4.0))
    inverse = 1.0 / rho
    kappa = 1.0 / (scale * (inverse - rho))
    rho, inverse, kappa = (t.astype(np.float32) for t in (rho, inverse, kappa))
    rho_slab = (rho.astype(np.float64) ** block).astype(np.float32)
    rounds = 1
    while np.float32(float(rho.max()) ** (block * rounds)) > 0:
        rounds += 1

    depth_table = left_table(sine)
    x_table = right_table(sine)
    y_table = left_table(sine[:, order])
    back_table = left_table(sine[order, :])
    x_low_table = right_table(sine[:, :coarse])
    low_table = left_table(sine[:coarse, :])
    eigen = (DIFFUSION * (fine_w[:, None] + fine_w[None, :])).astype(np.float32)
    coarse_eigen = (0.25 * DIFFUSION * (coarse_w[:, None] + coarse_w[None, :])).astype(np.float32)
    fine_own = lax.dynamic_slice(jnp.asarray((DIFFUSION * fine_w[order]).astype(np.float32)), (group_index * block,), (block,))
    coarse_own = lax.dynamic_slice(
        jnp.asarray((0.25 * DIFFUSION * coarse_w).astype(np.float32)), (group_index * half,), (half,)
    )

    previous = shifted(end_modes[0], "tm", 1)
    rows_spec = pl.BlockSpec((grid, ROWS, grid), lambda i: (0, i, 0))
    table_spec = whole_block(depth_table.shape)
    outgoing = call(
        depth_kernel,
        "depth",
        (block // ROWS,),
        [SMEM, table_spec, rows_spec, rows_spec],
        rows_spec,
        jax.ShapeDtypeStruct((grid, block, grid), F32),
        flops=6 * unit * grid,
        moved=12 * unit,
    )(first, depth_table, initial_modes, previous)
    modes = exchange(outgoing).reshape(groups, block, block, grid)
    start_low = jnp.where(is_first, initial_modes[:coarse, :half, :coarse], previous[:coarse, :half, :coarse])

    steps = block // planes
    pair = (2, grid, grid)
    pair_spec = whole_block(pair)
    back = lambda i: (0, steps - 1 - i, 0, 0)
    low, high, v, to_right, to_left = call(
        functools.partial(start_kernel, planes),
        "start",
        (steps,),
        [
            pl.BlockSpec((groups, planes, block, grid), back),
            whole_block(x_table.shape),
            table_spec,
            table_spec,
            pair_spec,
        ],
        [
            pl.BlockSpec((groups, planes, half, grid), back),
            pl.BlockSpec((groups, planes, half, grid), back),
            pl.BlockSpec((2, planes, grid, grid), back),
            pair_spec,
            pair_spec,
        ],
        [
            jax.ShapeDtypeStruct((groups, block, half, grid), F32),
            jax.ShapeDtypeStruct((groups, block, half, grid), F32),
            jax.ShapeDtypeStruct((2, block, grid, grid), F32),
            jax.ShapeDtypeStruct(pair, F32),
            jax.ShapeDtypeStruct(pair, F32),
        ],
        scratch=[pltpu.VMEM(pair, F32)],
        flops=24 * unit * grid,
        moved=16 * unit,
    )(modes, x_table, y_table, back_table, rho)
    low_back = exchange(low.reshape(grid, half, grid))

    from_left = jnp.zeros(pair, F32)
    from_right = jnp.zeros(pair, F32)
    for _ in range(rounds):
        rightward = to_right + rho_slab * from_left
        leftward = to_left + rho_slab * from_right
        from_left = jnp.where(group_index == 0, -rho * leftward, shifted(rightward, "gx", 1))
        from_right = jnp.where(group_index == groups - 1, -rho * rightward, shifted(leftward, "gx", -1))

    ahead = lambda i: (0, i, 0, 0)
    cubic = call(
        functools.partial(node_kernel, planes, block),
        "nodes",
        (steps,),
        [
            pl.BlockSpec((groups, planes, block, grid), ahead),
            pl.BlockSpec((groups, planes, half, grid), ahead),
            pl.BlockSpec((groups, planes, half, grid), ahead),
            pl.BlockSpec((2, planes, grid, grid), ahead),
            pair_spec,
            pair_spec,
            pair_spec,
            pair_spec,
            pair_spec,
            whole_block(x_table.shape),
            table_spec,
            whole_block(x_low_table.shape),
            whole_block(low_table.shape),
        ],
        pl.BlockSpec((groups, planes, half, coarse), ahead),
        jax.ShapeDtypeStruct((groups, block, half, coarse), F32),
        scratch=[pltpu.VMEM(pair, F32), pltpu.VMEM(pair, F32)],
        flops=28 * unit * grid,
        moved=17 * unit,
    )(modes, low, high, v, from_left, from_right, rho, inverse, kappa, x_table, y_table, x_low_table, low_table)
    cubic, high = lax.optimization_barrier((cubic, high))
    cubic_back = exchange(cubic.reshape(grid, half, coarse))
    high_back = exchange(high.reshape(grid, half, grid))

    low_spec = pl.BlockSpec((coarse, ROWS, coarse), lambda i: (0, i, 0))
    eigen_spec = whole_block(eigen.shape)
    coarse_eigen_spec = whole_block(coarse_eigen.shape)
    corner = jax.ShapeDtypeStruct((coarse, half, coarse), F32)
    result, gathered = call(
        functools.partial(low_kernel, factor),
        "low",
        (half // ROWS,),
        [SMEM, SMEM, table_spec, eigen_spec, coarse_eigen_spec, rows_spec, low_spec],
        [rows_spec, low_spec],
        [jax.ShapeDtypeStruct((grid, block, grid), F32), corner],
        flops=3 * unit * grid,
        moved=5 * unit,
    )(fine_own, coarse_own, depth_table, eigen, coarse_eigen, low_back, start_low)
    offset = call(
        functools.partial(offset_kernel, factor),
        "offset",
        (half // ROWS,),
        [
            SMEM,
            SMEM,
            whole_block(low_table.shape),
            coarse_eigen_spec,
            pl.BlockSpec((grid, ROWS, coarse), lambda i: (0, i, 0)),
            low_spec,
            low_spec,
        ],
        low_spec,
        corner,
        flops=unit * grid,
        moved=2 * unit,
    )(first, coarse_own, low_table, coarse_eigen, cubic_back, gathered, start_low)

    decay = 1.0 / (1.0 + coarse_eigen[:, None, :] + coarse_own[None, :, None])
    coarse_end = offset
    for _ in range(lax.axis_size("tm") - 1):
        coarse_end = jnp.where(is_first, offset, decay * shifted(coarse_end, "tm", 1) + offset)
    result = result.at[:coarse, :half, :coarse].set(coarse_end / factor)
    result = call(
        high_kernel,
        "high",
        (half // ROWS,),
        [SMEM, table_spec, eigen_spec, rows_spec, pl.BlockSpec(memory_space=pl.ANY)],
        pl.BlockSpec((grid, ROWS, grid), lambda i: (0, half // ROWS + i, 0)),
        jax.ShapeDtypeStruct((grid, block, grid), F32),
        flops=3 * unit * grid,
        moved=5 * unit,
        aliases={4: 0},
    )(fine_own[half:], depth_table, eigen, high_back, result)
    return (result[None], coarse_end[None])


def solution(mesh):
    return jax.shard_map(
        per_device,
        mesh=mesh,
        in_specs=(P("tm", None, "gx", None), P(None, "gx", None)),
        out_specs=(P("tm", None, "gx", None), P("tm", None, "gx", None)),
        check_vma=False,
    )
```

```python
import functools
import math

import jax
import jax.numpy as jnp
import ml_dtypes
import numpy as np
from jax import lax
from jax.experimental import pallas as pl
from jax.experimental.pallas import tpu as pltpu
from jax.sharding import PartitionSpec as P

DIFFUSION = 0.25
BF16 = jnp.bfloat16
F32 = jnp.float32
ROWS = 8
VMEM_BYTES = 56 * 1024 * 1024


def sine_matrix(length):
    index = np.arange(1, length + 1)
    phase = np.outer(index, index) % (2 * (length + 1))
    return np.sin(phase * (math.pi / (length + 1))) * math.sqrt(2.0 / (length + 1))


def omega(count):
    return 2.0 - 2.0 * np.cos((np.arange(count) + 1.0) * (math.pi / (count + 1)))


def fine_order(grid, groups):
    block, coarse = grid // groups, grid // 2
    half = block // 2
    position = np.arange(grid)
    within, group = position % block, position // block
    return np.where(within < half, group * half + within, coarse + group * half + within - half)


def halves(table):
    high = table.astype(ml_dtypes.bfloat16)
    low = (table - high.astype(np.float64)).astype(ml_dtypes.bfloat16)
    return high, low


def left_table(table):
    high, low = halves(table)
    return np.concatenate([high, high, low], axis=1)


def right_table(table):
    high, low = halves(table)
    return np.concatenate([high, high, low], axis=0)


def split3(value, axis):
    high = value.astype(BF16)
    low = (value - high.astype(F32)).astype(BF16)
    return jnp.concatenate([high, low, high], axis=axis)


def left(table, value):
    return jnp.dot(table, split3(value, 0), preferred_element_type=F32)


def right(value, table):
    return jnp.dot(split3(value, 1), table, preferred_element_type=F32)


def cube(value):
    return value * value * value


def whole_block(shape):
    return pl.BlockSpec(shape, lambda *_: (0,) * len(shape))


SMEM = pl.BlockSpec(memory_space=pltpu.SMEM)


def call(kernel, name, grid, in_specs, out_specs, out_shape, scratch=(), flops=0, moved=0, aliases=None):
    return pl.pallas_call(
        kernel,
        grid=grid,
        in_specs=in_specs,
        out_specs=out_specs,
        out_shape=out_shape,
        scratch_shapes=list(scratch),
        input_output_aliases=aliases or {},
        compiler_params=pltpu.CompilerParams(vmem_limit_bytes=VMEM_BYTES),
        cost_estimate=pl.CostEstimate(flops=flops, bytes_accessed=moved, transcendentals=0),
        name=name,
    )


def depth_kernel(first_ref, table_ref, initial_ref, previous_ref, out_ref):
    value = jnp.where(first_ref[0] == 1, initial_ref[...], previous_ref[...])
    value = jnp.swapaxes(value, 0, 1)
    rows = [left(table_ref[...], value[row]) for row in range(ROWS)]
    out_ref[...] = jnp.swapaxes(jnp.stack(rows), 0, 1)


def start_kernel(planes, modes_ref, sx_ref, sy_ref, syt_ref, rho_ref,
                 low_ref, high_ref, v_ref, to_right_ref, to_left_ref, power, cubic):
    step = pl.program_id(0)

    @pl.when(step == 0)
    def _():
        power[...] = jnp.ones_like(power)
        to_right_ref[...] = jnp.zeros_like(to_right_ref)
        to_left_ref[...] = jnp.zeros_like(to_left_ref)

    groups, _, block, wide = modes_ref.shape
    grid = groups * block
    half = block // 2
    modes = [modes_ref[:, j].reshape(grid, wide) for j in range(planes)]
    along_x = right(jnp.concatenate(modes, axis=0), sx_ref[...])
    terms = [cube(left(sy_ref[...], along_x[j * grid:(j + 1) * grid])) for j in range(planes)]
    along_x = right(jnp.concatenate(terms, axis=0), sx_ref[...])
    for j in range(planes):
        cubic[j] = left(syt_ref[...], along_x[j * grid:(j + 1) * grid])
    for strip in range(2 * groups):
        group, upper = strip // 2, strip % 2
        rows = slice(strip * half, (strip + 1) * half)
        within = slice(upper * half, (upper + 1) * half)
        out_ref = high_ref if upper else low_ref
        rho = [rho_ref[node, rows] for node in range(2)]
        carried = [to_left_ref[node, rows] for node in range(2)]
        weight = [power[node, rows] for node in range(2)]
        total = [to_right_ref[node, rows] for node in range(2)]
        for j in reversed(range(planes)):
            mode = modes_ref[group, j, within]
            source = 2.0 * mode - cubic[j, rows]
            out_ref[group, j] = source
            for node, value in enumerate((source, 0.5 * (mode + source))):
                carried[node] = value + rho[node] * carried[node]
                v_ref[node, j, rows] = carried[node]
                total[node] += weight[node] * value
                weight[node] = weight[node] * rho[node]
        for node in range(2):
            to_left_ref[node, rows] = carried[node]
            power[node, rows] = weight[node]
            to_right_ref[node, rows] = total[node]


def node_kernel(planes, slab, modes_ref, low_ref, high_ref, v_ref, from_left_ref, from_right_ref,
                rho_ref, inverse_ref, kappa_ref, sx_ref, sy_ref, sxl_ref, syl_ref,
                out_ref, left_sum, right_sum, nodes):
    step = pl.program_id(0)

    @pl.when(step == 0)
    def _():
        left_sum[...] = from_left_ref[...]

    @pl.when(step * planes % ROWS == 0)
    def _():
        rho = rho_ref[...]
        twice = rho * rho
        four = twice * twice
        eight = four * four
        right_sum[...] = lax.fori_loop(
            0, slab // ROWS - step * planes // ROWS, lambda _, total: total * eight, from_right_ref[...]
        )

    groups, _, block, wide = modes_ref.shape
    grid = groups * block
    half = block // 2
    for strip in range(2 * groups):
        group, upper = strip // 2, strip % 2
        rows = slice(strip * half, (strip + 1) * half)
        within = slice(upper * half, (upper + 1) * half)
        source_ref = high_ref if upper else low_ref
        rho = [rho_ref[node, rows] for node in range(2)]
        inverse = [inverse_ref[node, rows] for node in range(2)]
        kappa = [kappa_ref[node, rows] for node in range(2)]
        before = [left_sum[node, rows] for node in range(2)]
        after = [right_sum[node, rows] for node in range(2)]
        for j in range(planes):
            source = source_ref[group, j]
            for node, value in enumerate((source, 0.5 * (modes_ref[group, j, within] + source))):
                behind = rho[node] * before[node]
                before[node] = value + behind
                nodes[node, j, rows] = kappa[node] * (behind + v_ref[node, j, rows] + after[node])
                after[node] = after[node] * inverse[node]
        for node in range(2):
            left_sum[node, rows] = before[node]
            right_sum[node, rows] = after[node]
    along_x = right(nodes[...].reshape(2 * planes * grid, wide), sx_ref[...])
    fields = [left(sy_ref[...], along_x[j * grid:(j + 1) * grid]) for j in range(2 * planes)]
    terms = [cube(fields[j]) + 4.0 * cube(fields[planes + j]) for j in range(planes)]
    along_x = right(jnp.concatenate(terms, axis=0), sxl_ref[...])
    for j in range(planes):
        term = left(syl_ref[...], along_x[j * grid:(j + 1) * grid])
        out_ref[:, j] = term.reshape(groups, half, wide // 2)


def low_kernel(factor, fine_ref, coarse_ref, table_ref, eigen_ref, coarse_eigen_ref, source_ref, start_ref,
               out_ref, gathered_ref):
    base = pl.program_id(0) * ROWS
    coarse = start_ref.shape[0]
    sources = jnp.swapaxes(source_ref[...], 0, 1)
    starts = jnp.swapaxes(start_ref[...], 0, 1)
    ends, gathered = [], []
    for row in range(ROWS):
        source = left(table_ref[...], sources[row])
        eigen = eigen_ref[...] + fine_ref[base + row]
        node_end = source / (1.0 + eigen)
        ends.append(node_end)
        source, node_end, eigen = source[:coarse, :coarse], node_end[:coarse, :coarse], eigen[:coarse, :coarse]
        start = starts[row]
        node_mid = 0.5 * (start + source) / (1.0 + 0.5 * eigen)
        rate = source - (1.0 + eigen) * start + (1.0 - eigen) * (4.0 * node_mid + node_end)
        coarse_eigen = coarse_eigen_ref[...] + coarse_ref[base + row]
        gathered.append(factor * (rate / 6.0 + coarse_eigen * node_end))
    out_ref[...] = jnp.swapaxes(jnp.stack(ends), 0, 1)
    gathered_ref[...] = jnp.swapaxes(jnp.stack(gathered), 0, 1)


def offset_kernel(factor, first_ref, coarse_ref, table_ref, coarse_eigen_ref, cubic_ref, gathered_ref, start_ref,
                  out_ref):
    base = pl.program_id(0) * ROWS
    first = first_ref[0] == 1
    cubics = jnp.swapaxes(cubic_ref[...], 0, 1)
    given = jnp.swapaxes(gathered_ref[...] + jnp.where(first, factor * start_ref[...], 0.0), 0, 1)
    rows = []
    for row in range(ROWS):
        total = given[row] - (factor / 6.0) * left(table_ref[...], cubics[row])
        rows.append(total / (1.0 + coarse_eigen_ref[...] + coarse_ref[base + row]))
    out_ref[...] = jnp.swapaxes(jnp.stack(rows), 0, 1)


def high_kernel(fine_ref, table_ref, eigen_ref, source_ref, _, out_ref):
    base = pl.program_id(0) * ROWS
    sources = jnp.swapaxes(source_ref[...], 0, 1)
    rows = []
    for row in range(ROWS):
        source = left(table_ref[...], sources[row])
        rows.append(source / (1.0 + eigen_ref[...] + fine_ref[base + row]))
    out_ref[...] = jnp.swapaxes(jnp.stack(rows), 0, 1)


def shifted(value, axis, by):
    length = lax.axis_size(axis)
    pairs = [(i, i + by) for i in range(length) if 0 <= i + by < length]
    return lax.ppermute(value, axis, pairs)


def exchange(value):
    return lax.all_to_all(value, "gx", split_axis=0, concat_axis=0, tiled=True)


def per_device(end_modes, initial_modes):
    grid = initial_modes.shape[0]
    coarse = grid // 2
    groups = lax.axis_size("gx")
    block = grid // groups
    half = block // 2
    planes = 4
    slice_index = lax.axis_index("tm")
    group_index = lax.axis_index("gx")
    is_first = slice_index == 0
    first = is_first.astype(jnp.int32)[None]
    order = fine_order(grid, groups)
    sine = sine_matrix(grid)
    fine_w, coarse_w = omega(grid), omega(coarse)
    factor = ((coarse + 1) / (grid + 1)) ** 1.5
    unit = grid * block * grid

    flat = fine_w[order][:, None] + fine_w[None, :]
    scale = np.array([1.0, 0.5])[:, None, None] * DIFFUSION
    diagonal = 1.0 / scale + 2.0 + flat[None]
    rho = 2.0 / (diagonal + np.sqrt(diagonal * diagonal - 4.0))
    inverse = 1.0 / rho
    kappa = 1.0 / (scale * (inverse - rho))
    rho, inverse, kappa = (t.astype(np.float32) for t in (rho, inverse, kappa))
    rho_slab = (rho.astype(np.float64) ** block).astype(np.float32)
    rounds = 1
    while np.float32(float(rho.max()) ** (block * rounds)) > 0:
        rounds += 1

    depth_table = left_table(sine)
    x_table = right_table(sine)
    y_table = left_table(sine[:, order])
    back_table = left_table(sine[order, :])
    x_low_table = right_table(sine[:, :coarse])
    low_table = left_table(sine[:coarse, :])
    eigen = (DIFFUSION * (fine_w[:, None] + fine_w[None, :])).astype(np.float32)
    coarse_eigen = (0.25 * DIFFUSION * (coarse_w[:, None] + coarse_w[None, :])).astype(np.float32)
    fine_own = lax.dynamic_slice(jnp.asarray((DIFFUSION * fine_w[order]).astype(np.float32)), (group_index * block,), (block,))
    coarse_own = lax.dynamic_slice(
        jnp.asarray((0.25 * DIFFUSION * coarse_w).astype(np.float32)), (group_index * half,), (half,)
    )

    previous = shifted(end_modes[0], "tm", 1)
    rows_spec = pl.BlockSpec((grid, ROWS, grid), lambda i: (0, i, 0))
    table_spec = whole_block(depth_table.shape)
    outgoing = call(
        depth_kernel,
        "depth",
        (block // ROWS,),
        [SMEM, table_spec, rows_spec, rows_spec],
        rows_spec,
        jax.ShapeDtypeStruct((grid, block, grid), F32),
        flops=6 * unit * grid,
        moved=12 * unit,
    )(first, depth_table, initial_modes, previous)
    modes = exchange(outgoing).reshape(groups, block, block, grid)
    start_low = jnp.where(is_first, initial_modes[:coarse, :half, :coarse], previous[:coarse, :half, :coarse])

    steps = block // planes
    pair = (2, grid, grid)
    pair_spec = whole_block(pair)
    back = lambda i: (0, steps - 1 - i, 0, 0)
    low, high, v, to_right, to_left = call(
        functools.partial(start_kernel, planes),
        "start",
        (steps,),
        [
            pl.BlockSpec((groups, planes, block, grid), back),
            whole_block(x_table.shape),
            table_spec,
            table_spec,
            pair_spec,
        ],
        [
            pl.BlockSpec((groups, planes, half, grid), back),
            pl.BlockSpec((groups, planes, half, grid), back),
            pl.BlockSpec((2, planes, grid, grid), back),
            pair_spec,
            pair_spec,
        ],
        [
            jax.ShapeDtypeStruct((groups, block, half, grid), F32),
            jax.ShapeDtypeStruct((groups, block, half, grid), F32),
            jax.ShapeDtypeStruct((2, block, grid, grid), F32),
            jax.ShapeDtypeStruct(pair, F32),
            jax.ShapeDtypeStruct(pair, F32),
        ],
        scratch=[pltpu.VMEM(pair, F32), pltpu.VMEM((planes, grid, grid), F32)],
        flops=24 * unit * grid,
        moved=16 * unit,
    )(modes, x_table, y_table, back_table, rho)
    low_back = exchange(low.reshape(grid, half, grid))

    from_left = jnp.zeros(pair, F32)
    from_right = jnp.zeros(pair, F32)
    for _ in range(rounds):
        rightward = to_right + rho_slab * from_left
        leftward = to_left + rho_slab * from_right
        from_left = jnp.where(group_index == 0, -rho * leftward, shifted(rightward, "gx", 1))
        from_right = jnp.where(group_index == groups - 1, -rho * rightward, shifted(leftward, "gx", -1))

    ahead = lambda i: (0, i, 0, 0)
    cubic = call(
        functools.partial(node_kernel, planes, block),
        "nodes",
        (steps,),
        [
            pl.BlockSpec((groups, planes, block, grid), ahead),
            pl.BlockSpec((groups, planes, half, grid), ahead),
            pl.BlockSpec((groups, planes, half, grid), ahead),
            pl.BlockSpec((2, planes, grid, grid), ahead),
            pair_spec,
            pair_spec,
            pair_spec,
            pair_spec,
            pair_spec,
            whole_block(x_table.shape),
            table_spec,
            whole_block(x_low_table.shape),
            whole_block(low_table.shape),
        ],
        pl.BlockSpec((groups, planes, half, coarse), ahead),
        jax.ShapeDtypeStruct((groups, block, half, coarse), F32),
        scratch=[pltpu.VMEM(pair, F32), pltpu.VMEM(pair, F32), pltpu.VMEM((2, planes, grid, grid), F32)],
        flops=28 * unit * grid,
        moved=17 * unit,
    )(modes, low, high, v, from_left, from_right, rho, inverse, kappa, x_table, y_table, x_low_table, low_table)
    cubic, high, low_back = lax.optimization_barrier((cubic, high, low_back))
    cubic_back = exchange(cubic.reshape(grid, half, coarse))
    high_back = exchange(high.reshape(grid, half, grid))

    low_spec = pl.BlockSpec((coarse, ROWS, coarse), lambda i: (0, i, 0))
    eigen_spec = whole_block(eigen.shape)
    coarse_eigen_spec = whole_block(coarse_eigen.shape)
    corner = jax.ShapeDtypeStruct((coarse, half, coarse), F32)
    result, gathered = call(
        functools.partial(low_kernel, factor),
        "low",
        (half // ROWS,),
        [SMEM, SMEM, table_spec, eigen_spec, coarse_eigen_spec, rows_spec, low_spec],
        [rows_spec, low_spec],
        [jax.ShapeDtypeStruct((grid, block, grid), F32), corner],
        flops=3 * unit * grid,
        moved=5 * unit,
    )(fine_own, coarse_own, depth_table, eigen, coarse_eigen, low_back, start_low)
    offset = call(
        functools.partial(offset_kernel, factor),
        "offset",
        (half // ROWS,),
        [
            SMEM,
            SMEM,
            whole_block(low_table.shape),
            coarse_eigen_spec,
            pl.BlockSpec((grid, ROWS, coarse), lambda i: (0, i, 0)),
            low_spec,
            low_spec,
        ],
        low_spec,
        corner,
        flops=unit * grid,
        moved=2 * unit,
    )(first, coarse_own, low_table, coarse_eigen, cubic_back, gathered, start_low)

    decay = 1.0 / (1.0 + coarse_eigen[:, None, :] + coarse_own[None, :, None])
    coarse_end = offset
    for _ in range(lax.axis_size("tm") - 1):
        coarse_end = jnp.where(is_first, offset, decay * shifted(coarse_end, "tm", 1) + offset)
    result = result.at[:coarse, :half, :coarse].set(coarse_end / factor)
    result = call(
        high_kernel,
        "high",
        (half // ROWS,),
        [SMEM, table_spec, eigen_spec, rows_spec, pl.BlockSpec(memory_space=pl.ANY)],
        pl.BlockSpec((grid, ROWS, grid), lambda i: (0, half // ROWS + i, 0)),
        jax.ShapeDtypeStruct((grid, block, grid), F32),
        flops=3 * unit * grid,
        moved=5 * unit,
        aliases={4: 0},
    )(fine_own[half:], depth_table, eigen, high_back, result)
    return (result[None], coarse_end[None])


def solution(mesh):
    return jax.shard_map(
        per_device,
        mesh=mesh,
        in_specs=(P("tm", None, "gx", None), P(None, "gx", None)),
        out_specs=(P("tm", None, "gx", None), P("tm", None, "gx", None)),
        check_vma=False,
    )
```

```python
import functools
import math

import jax
import jax.numpy as jnp
import ml_dtypes
import numpy as np
from jax import lax
from jax.experimental import pallas as pl
from jax.experimental.pallas import tpu as pltpu
from jax.sharding import PartitionSpec as P

DIFFUSION = 0.25
BF16 = jnp.bfloat16
F32 = jnp.float32
ROWS = 8
VMEM_BYTES = 56 * 1024 * 1024


def sine_matrix(length):
    index = np.arange(1, length + 1)
    phase = np.outer(index, index) % (2 * (length + 1))
    return np.sin(phase * (math.pi / (length + 1))) * math.sqrt(2.0 / (length + 1))


def omega(count):
    return 2.0 - 2.0 * np.cos((np.arange(count) + 1.0) * (math.pi / (count + 1)))


def fine_order(grid, groups):
    block, coarse = grid // groups, grid // 2
    half = block // 2
    position = np.arange(grid)
    within, group = position % block, position // block
    return np.where(within < half, group * half + within, coarse + group * half + within - half)


def halves(table):
    high = table.astype(ml_dtypes.bfloat16)
    low = (table - high.astype(np.float64)).astype(ml_dtypes.bfloat16)
    return high, low


def left_table(table):
    high, low = halves(table)
    return np.concatenate([high, high, low], axis=1)


def right_table(table):
    high, low = halves(table)
    return np.concatenate([high, high, low], axis=0)


def split3(value, axis):
    high = value.astype(BF16)
    low = (value - high.astype(F32)).astype(BF16)
    return jnp.concatenate([high, low, high], axis=axis)


def left(table, value):
    return jnp.dot(table, split3(value, 0), preferred_element_type=F32)


def right(value, table):
    return jnp.dot(split3(value, 1), table, preferred_element_type=F32)


def cube(value):
    return value * value * value


def whole_block(shape):
    return pl.BlockSpec(shape, lambda *_: (0,) * len(shape))


SMEM = pl.BlockSpec(memory_space=pltpu.SMEM)


def call(kernel, name, grid, in_specs, out_specs, out_shape, scratch=(), flops=0, moved=0, aliases=None):
    return pl.pallas_call(
        kernel,
        grid=grid,
        in_specs=in_specs,
        out_specs=out_specs,
        out_shape=out_shape,
        scratch_shapes=list(scratch),
        input_output_aliases=aliases or {},
        compiler_params=pltpu.CompilerParams(vmem_limit_bytes=VMEM_BYTES),
        cost_estimate=pl.CostEstimate(flops=flops, bytes_accessed=moved, transcendentals=0),
        name=name,
    )


def depth_kernel(last_ref, table_ref, initial_ref, end_ref, *out_refs):
    value = jnp.swapaxes(jnp.where(last_ref[0] == 1, initial_ref[...], end_ref[0]), 0, 1)
    rows = jnp.stack([left(table_ref[...], value[row]) for row in range(ROWS)])
    groups, _, _, wide = out_refs[0].shape
    rows = jnp.swapaxes(rows, 0, 1).reshape(groups, -1, ROWS, wide)
    begin = 0
    for out_ref in out_refs:
        planes = out_ref.shape[1]
        out_ref[...] = rows[:, begin:begin + planes]
        begin += planes


def start_kernel(planes, modes_ref, sx_ref, sy_ref, syt_ref, rho_ref, power_ref, right_ref, left_ref, *refs):
    corner_ref, side_ref, high_ref, v_ref, power, to_right_ref, to_left_ref, cubic = refs[-8:]

    @pl.when(pl.program_id(0) == 0)
    def _():
        power[...] = power_ref[...]
        to_right_ref[...] = right_ref[...]
        to_left_ref[...] = left_ref[...]

    groups, _, block, wide = modes_ref.shape
    grid = groups * block
    half = block // 2
    modes = [modes_ref[:, j].reshape(grid, wide) for j in range(planes)]
    along_x = right(jnp.concatenate(modes, axis=0), sx_ref[...])
    terms = [cube(left(sy_ref[...], along_x[j * grid:(j + 1) * grid])) for j in range(planes)]
    along_x = right(jnp.concatenate(terms, axis=0), sx_ref[...])
    for j in range(planes):
        cubic[j] = left(syt_ref[...], along_x[j * grid:(j + 1) * grid])
    for strip in range(2 * groups):
        group, upper = strip // 2, strip % 2
        rows = slice(strip * half, (strip + 1) * half)
        within = slice(upper * half, (upper + 1) * half)
        rho = [rho_ref[node, rows] for node in range(2)]
        carried = [to_left_ref[node, rows] for node in range(2)]
        weight = [power[node, rows] for node in range(2)]
        total = [to_right_ref[node, rows] for node in range(2)]
        for j in reversed(range(planes)):
            mode = modes_ref[group, j, within]
            source = 2.0 * mode - cubic[j, rows]
            if upper:
                high_ref[group, j] = source
            else:
                corner_ref[group, j] = source[:, :wide // 2]
                side_ref[group, j] = source[:, wide // 2:]
            for node, value in enumerate((source, 0.5 * (mode + source))):
                carried[node] = value + rho[node] * carried[node]
                v_ref[node, j, rows] = carried[node]
                v_ref[2 + node, j, rows] = value
                total[node] += weight[node] * value
                weight[node] = weight[node] * rho[node]
        for node in range(2):
            to_left_ref[node, rows] = carried[node]
            power[node, rows] = weight[node]
            to_right_ref[node, rows] = total[node]


def node_kernel(planes, slab, v_ref, from_left_ref, from_right_ref, rho_ref, inverse_ref, kappa_ref,
                sx_ref, sy_ref, sxl_ref, syl_ref, out_ref, left_sum, right_sum, nodes):
    step = pl.program_id(0)
    plane = step * planes

    @pl.when(step == 0)
    def _():
        left_sum[...] = from_left_ref[...]

    @pl.when(plane % ROWS == 0)
    def _():
        rho = rho_ref[...]
        twice = rho * rho
        four = twice * twice
        eight = four * four
        right_sum[...] = lax.fori_loop(
            0, slab // ROWS - plane // ROWS, lambda _, total: total * eight, from_right_ref[...]
        )

    groups, _, half, low = out_ref.shape
    grid = v_ref.shape[2]
    wide = v_ref.shape[3]
    for strip in range(2 * groups):
        rows = slice(strip * half, (strip + 1) * half)
        rho = [rho_ref[node, rows] for node in range(2)]
        inverse = [inverse_ref[node, rows] for node in range(2)]
        kappa = [kappa_ref[node, rows] for node in range(2)]
        before = [left_sum[node, rows] for node in range(2)]
        after = [right_sum[node, rows] for node in range(2)]
        for j in range(planes):
            for node in range(2):
                behind = rho[node] * before[node]
                before[node] = v_ref[2 + node, j, rows] + behind
                nodes[node, j, rows] = kappa[node] * (behind + v_ref[node, j, rows] + after[node])
                after[node] = after[node] * inverse[node]
        for node in range(2):
            left_sum[node, rows] = before[node]
            right_sum[node, rows] = after[node]
    along_x = right(nodes[...].reshape(2 * planes * grid, wide), sx_ref[...])
    fields = [left(sy_ref[...], along_x[j * grid:(j + 1) * grid]) for j in range(2 * planes)]
    terms = [cube(fields[j]) + 4.0 * cube(fields[planes + j]) for j in range(planes)]
    along_x = right(jnp.concatenate(terms, axis=0), sxl_ref[...])
    for j in range(planes):
        term = left(syl_ref[...], along_x[j * grid:(j + 1) * grid])
        out_ref[:, j] = term.reshape(groups, half, low)


def joined(refs):
    parts = [ref[...] for ref in refs]
    parts = jnp.concatenate(parts, axis=1)
    return parts.reshape(parts.shape[0] * parts.shape[1], *parts.shape[2:])


def low_kernel(factor, fine_ref, coarse_ref, table_ref, eigen_ref, coarse_eigen_ref, corner_ref, start_ref,
               out_ref, gathered_ref):
    base = pl.program_id(0) * ROWS
    coarse = start_ref.shape[0]
    sources = jnp.swapaxes(corner_ref[...], 0, 1)
    starts = jnp.swapaxes(start_ref[...], 0, 1)
    ends, gathered = [], []
    for row in range(ROWS):
        source = left(table_ref[...], sources[row])
        eigen = eigen_ref[...] + fine_ref[base + row]
        node_end = source / (1.0 + eigen)
        ends.append(node_end)
        source, node_end, eigen = source[:coarse], node_end[:coarse], eigen[:coarse]
        start = starts[row]
        node_mid = 0.5 * (start + source) / (1.0 + 0.5 * eigen)
        rate = source - (1.0 + eigen) * start + (1.0 - eigen) * (4.0 * node_mid + node_end)
        coarse_eigen = coarse_eigen_ref[...] + coarse_ref[base + row]
        gathered.append(factor * (rate / 6.0 + coarse_eigen * node_end))
    out_ref[...] = jnp.swapaxes(jnp.stack(ends), 0, 1)
    gathered_ref[...] = jnp.swapaxes(jnp.stack(gathered), 0, 1)


def offset_kernel(factor, first_ref, coarse_ref, table_ref, coarse_eigen_ref, gathered_ref, start_ref, cubic_ref,
                  out_ref):
    base = pl.program_id(0) * ROWS
    first = first_ref[0] == 1
    cubics = jnp.swapaxes(cubic_ref[...], 0, 1)
    given = jnp.swapaxes(gathered_ref[...] + jnp.where(first, factor * start_ref[...], 0.0), 0, 1)
    rows = []
    for row in range(ROWS):
        total = given[row] - (factor / 6.0) * left(table_ref[...], cubics[row])
        rows.append(total / (1.0 + coarse_eigen_ref[...] + coarse_ref[base + row]))
    out_ref[...] = jnp.swapaxes(jnp.stack(rows), 0, 1)


def finish_kernel(fine_ref, table_ref, eigen_ref, *refs):
    base = pl.program_id(0) * ROWS
    out_ref = refs[-1]
    sources = jnp.swapaxes(joined(refs[:-2]), 0, 1)
    rows = []
    for row in range(ROWS):
        source = left(table_ref[...], sources[row])
        rows.append(source / (1.0 + eigen_ref[...] + fine_ref[base + row]))
    out_ref[...] = jnp.swapaxes(jnp.stack(rows), 0, 1)


def shifted(value, axis, by):
    length = lax.axis_size(axis)
    pairs = [(i, i + by) for i in range(length) if 0 <= i + by < length]
    return lax.ppermute(value, axis, pairs)


def turned(value, axis):
    length = lax.axis_size(axis)
    return lax.ppermute(value, axis, [(i, (i + 1) % length) for i in range(length)])


def exchange(value):
    return lax.all_to_all(value, "gx", split_axis=0, concat_axis=0, tiled=True)


def after(value, *earlier):
    return lax.optimization_barrier((value, *earlier))


def per_device(end_modes, initial_modes):
    grid = initial_modes.shape[0]
    coarse = grid // 2
    groups = lax.axis_size("gx")
    block = grid // groups
    half = block // 2
    planes = 4
    slice_index = lax.axis_index("tm")
    group_index = lax.axis_index("gx")
    is_first = slice_index == 0
    slices = lax.axis_size("tm")
    first = is_first.astype(jnp.int32)[None]
    last = (slice_index == slices - 1).astype(jnp.int32)[None]
    order = fine_order(grid, groups)
    sine = sine_matrix(grid)
    fine_w, coarse_w = omega(grid), omega(coarse)
    factor = ((coarse + 1) / (grid + 1)) ** 1.5
    unit = grid * block * grid

    flat = fine_w[order][:, None] + fine_w[None, :]
    scale = np.array([1.0, 0.5])[:, None, None] * DIFFUSION
    diagonal = 1.0 / scale + 2.0 + flat[None]
    rho = 2.0 / (diagonal + np.sqrt(diagonal * diagonal - 4.0))
    inverse = 1.0 / rho
    kappa = 1.0 / (scale * (inverse - rho))
    rho, inverse, kappa = (t.astype(np.float32) for t in (rho, inverse, kappa))
    rho_slab = (rho.astype(np.float64) ** block).astype(np.float32)
    rounds = 1
    while np.float32(float(rho.max()) ** (block * rounds)) > 0:
        rounds += 1

    depth_table = left_table(sine)
    x_table = right_table(sine)
    y_table = left_table(sine[:, order])
    back_table = left_table(sine[order, :])
    x_low_table = right_table(sine[:, :coarse])
    low_table = left_table(sine[:coarse, :])
    eigen = (DIFFUSION * (fine_w[:, None] + fine_w[None, :])).astype(np.float32)
    coarse_eigen = (0.25 * DIFFUSION * (coarse_w[:, None] + coarse_w[None, :])).astype(np.float32)
    fine_own = lax.dynamic_slice(jnp.asarray((DIFFUSION * fine_w[order]).astype(np.float32)), (group_index * block,), (block,))
    coarse_own = lax.dynamic_slice(
        jnp.asarray((0.25 * DIFFUSION * coarse_w).astype(np.float32)), (group_index * half,), (half,)
    )

    rows_spec = pl.BlockSpec((grid, ROWS, grid), lambda i: (0, i, 0))
    table_spec = whole_block(depth_table.shape)
    quarter = block // 4
    middle = 3 * quarter // planes // 2 * planes
    lengths = (quarter, middle, block - quarter - middle)
    begins = (0, quarter, quarter + middle)
    parts = len(lengths)
    outgoing = call(
        depth_kernel,
        "depth",
        (block // ROWS,),
        [SMEM, table_spec, rows_spec, pl.BlockSpec((1, grid, ROWS, grid), lambda i: (0, 0, i, 0))],
        [pl.BlockSpec((groups, length, ROWS, grid), lambda i: (0, 0, i, 0)) for length in lengths],
        [jax.ShapeDtypeStruct((groups, length, block, grid), F32) for length in lengths],
        flops=6 * unit * grid,
        moved=12 * unit,
    )(last, depth_table, initial_modes, end_modes)

    pair = (2, grid, grid)
    pair_spec = whole_block(pair)
    whole = (groups, block, half)
    shapes = [
        (*whole, coarse),
        (*whole, coarse),
        (groups, block - lengths[0], half, grid),
        (4, block, grid, grid),
    ]
    arrays = None
    state = (np.ones(pair, np.float32), np.zeros(pair, np.float32), np.zeros(pair, np.float32))
    backs, states = {}, {}
    for part in reversed(range(parts)):
        given = outgoing[part]
        if part + 1 in backs:
            given, *_ = after(given, backs[part + 1], *states.get(part + 2, ()))
        backs[part] = exchange(given)
        modes = turned(backs[part], "tm")
        steps = lengths[part] // planes
        bases = [begins[part] // planes] * 4
        if part == 0:
            shapes[2] = (groups, lengths[0], half, grid)
        else:
            bases[2] = (begins[part] - lengths[0]) // planes
        specs = [
            pl.BlockSpec(
                (4, planes, grid, grid) if n == 3 else (groups, planes, half, shapes[n][3]),
                lambda i, base=base, steps=steps: (0, base + steps - 1 - i, 0, 0),
            )
            for n, base in enumerate(bases)
        ]
        held = [n for n in range(4) if arrays is not None and not (part == 0 and n == 2)]
        outs = call(
            functools.partial(start_kernel, planes),
            "start",
            (steps,),
            [
                pl.BlockSpec((groups, planes, block, grid), lambda i, steps=steps: (0, steps - 1 - i, 0, 0)),
                whole_block(x_table.shape),
                table_spec,
                table_spec,
                pair_spec,
                pair_spec,
                pair_spec,
                pair_spec,
            ] + [pl.BlockSpec(memory_space=pl.ANY)] * len(held),
            specs + [pair_spec] * 3,
            [jax.ShapeDtypeStruct(shape, F32) for shape in shapes] + [jax.ShapeDtypeStruct(pair, F32)] * 3,
            scratch=[pltpu.VMEM((planes, grid, grid), F32)],
            flops=24 * unit * grid * lengths[part] // block,
            moved=24 * unit * lengths[part] // block,
            aliases={8 + place: n for place, n in enumerate(held)},
        )(modes, x_table, y_table, back_table, rho, *state, *(arrays[n] for n in held))
        if part == 0:
            high_first = outs[2]
        else:
            high_rest = outs[2]
        arrays, state = outs[:4], outs[4:]
        states[part] = state
    corner, side, _, v = arrays
    _, to_right, to_left = state
    high_rest, backs[0] = after(high_rest, backs[0])
    high_rest_back = exchange(high_rest.reshape(-1, half, grid))
    at_start, at_end = group_index == 0, group_index == groups - 1
    if rounds <= 2:
        rightward = jnp.where(at_start, to_right - rho_slab * (rho * to_left), to_right)
        leftward = jnp.where(at_end, to_left - rho_slab * (rho * to_right), to_left)
        from_left = shifted(rightward, "gx", 1) + rho_slab * shifted(rightward, "gx", 2)
        from_right = shifted(leftward, "gx", -1) + rho_slab * shifted(leftward, "gx", -2)
        from_left, from_right = (
            jnp.where(at_start, -rho * (to_left + rho_slab * from_right), from_left),
            jnp.where(at_end, -rho * (to_right + rho_slab * from_left), from_right),
        )
    else:
        from_left = jnp.zeros(pair, F32)
        from_right = jnp.zeros(pair, F32)
        for _ in range(rounds):
            rightward = to_right + rho_slab * from_left
            leftward = to_left + rho_slab * from_right
            from_left = jnp.where(at_start, -rho * leftward, shifted(rightward, "gx", 1))
            from_right = jnp.where(at_end, -rho * rightward, shifted(leftward, "gx", -1))

    corner, high_rest_back, from_left, from_right = after(corner, high_rest_back, from_left, from_right)
    corner_back = exchange(corner.reshape(grid, half, coarse))
    cubic = call(
        functools.partial(node_kernel, planes, block),
        "nodes",
        (block // planes,),
        [pl.BlockSpec((4, planes, grid, grid), lambda i: (0, i, 0, 0))]
        + [pair_spec] * 5
        + [
            whole_block(x_table.shape),
            table_spec,
            whole_block(x_low_table.shape),
            whole_block(low_table.shape),
        ],
        pl.BlockSpec((groups, planes, half, coarse), lambda i: (0, i, 0, 0)),
        jax.ShapeDtypeStruct((groups, block, half, coarse), F32),
        scratch=[pltpu.VMEM(pair, F32), pltpu.VMEM(pair, F32), pltpu.VMEM((2, planes, grid, grid), F32)],
        flops=28 * unit * grid,
        moved=17 * unit,
    )(v, from_left, from_right, rho, inverse, kappa, x_table, y_table, x_low_table, low_table)
    cubic, corner_back = after(cubic, corner_back)
    cubic_back = exchange(cubic.reshape(grid, half, coarse))
    high_first, cubic_back = after(high_first, cubic_back)
    high_first_back = exchange(high_first.reshape(-1, half, grid))
    side, high_first_back = after(side, high_first_back)
    side_back = exchange(side.reshape(grid, half, coarse))
    high_backs = [part.reshape(groups, -1, half, grid) for part in (high_first_back, high_rest_back)]
    start_low = jnp.where(
        is_first, initial_modes[:coarse, :half, :coarse], shifted(end_modes[0, :coarse, :half, :coarse], "tm", 1)
    )

    low_spec = pl.BlockSpec((coarse, ROWS, coarse), lambda i: (0, i, 0))
    coarse_eigen_spec = whole_block(coarse_eigen.shape)
    quarter_spec = pl.BlockSpec((grid, ROWS, coarse), lambda i: (0, i, 0))
    corner_shape = jax.ShapeDtypeStruct((coarse, half, coarse), F32)
    result_shape = jax.ShapeDtypeStruct((grid, block, grid), F32)
    result, gathered = call(
        functools.partial(low_kernel, factor),
        "low",
        (half // ROWS,),
        [SMEM, SMEM, table_spec, whole_block((grid, coarse)), coarse_eigen_spec, quarter_spec, low_spec],
        [quarter_spec, low_spec],
        [result_shape, corner_shape],
        flops=2 * unit * grid,
        moved=3 * unit,
    )(fine_own, coarse_own, depth_table, eigen[:, :coarse], coarse_eigen, corner_back, start_low)
    offset = call(
        functools.partial(offset_kernel, factor),
        "offset",
        (half // ROWS,),
        [SMEM, SMEM, whole_block(low_table.shape), coarse_eigen_spec, low_spec, low_spec, quarter_spec],
        low_spec,
        corner_shape,
        flops=unit * grid,
        moved=2 * unit,
    )(first, coarse_own, low_table, coarse_eigen, gathered, start_low, cubic_back)

    def finish(result, sources, weights, eigen, row, column):
        width = eigen.shape[1]
        return call(
            finish_kernel,
            "finish",
            (half // ROWS,),
            [SMEM, table_spec, whole_block(eigen.shape)]
            + [pl.BlockSpec((groups, part.shape[1], ROWS, width), lambda i: (0, 0, i, 0)) for part in sources]
            + [pl.BlockSpec(memory_space=pl.ANY)],
            pl.BlockSpec((grid, ROWS, width), lambda i: (0, row // ROWS + i, column)),
            result_shape,
            flops=3 * unit * width,
            moved=5 * unit * width // grid,
            aliases={3 + len(sources): 0},
        )(weights, depth_table, eigen, *sources, result)

    result = finish(result, high_backs, fine_own[half:], eigen, half, 0)
    decay = 1.0 / (1.0 + coarse_eigen[:, None, :] + coarse_own[None, :, None])
    coarse_end = offset
    for turn in range(1, slices):
        incoming = lax.ppermute(coarse_end, "tm", [(turn - 1, turn)])
        coarse_end = jnp.where(slice_index == turn, decay * incoming + offset, coarse_end)
    result = result.at[:coarse, :half, :coarse].set(coarse_end / factor)
    result = finish(
        result, [side_back.reshape(groups, block, half, coarse)], fine_own[:half], eigen[:, coarse:], 0, 1
    )
    return (result[None], coarse_end[None])


def solution(mesh):
    return jax.shard_map(
        per_device,
        mesh=mesh,
        in_specs=(P("tm", None, "gx", None), P(None, "gx", None)),
        out_specs=(P("tm", None, "gx", None), P("tm", None, "gx", None)),
        check_vma=False,
    )
```

```python
import functools
import math

import jax
import jax.numpy as jnp
import ml_dtypes
import numpy as np
from jax import lax
from jax.experimental import pallas as pl
from jax.experimental.pallas import tpu as pltpu
from jax.sharding import PartitionSpec as P

DIFFUSION = 0.25
BF16 = jnp.bfloat16
F32 = jnp.float32
ROWS = 8
VMEM_BYTES = 56 * 1024 * 1024


def sine_matrix(length):
    index = np.arange(1, length + 1)
    phase = np.outer(index, index) % (2 * (length + 1))
    return np.sin(phase * (math.pi / (length + 1))) * math.sqrt(2.0 / (length + 1))


def omega(count):
    return 2.0 - 2.0 * np.cos((np.arange(count) + 1.0) * (math.pi / (count + 1)))


def fine_order(grid, groups):
    block, coarse = grid // groups, grid // 2
    half = block // 2
    position = np.arange(grid)
    within, group = position % block, position // block
    return np.where(within < half, group * half + within, coarse + group * half + within - half)


def halves(table):
    high = table.astype(ml_dtypes.bfloat16)
    low = (table - high.astype(np.float64)).astype(ml_dtypes.bfloat16)
    return high, low


def left_table(table):
    high, low = halves(table)
    return np.concatenate([high, high, low], axis=1)


def right_table(table):
    high, low = halves(table)
    return np.concatenate([high, high, low], axis=0)


def split3(value, axis):
    high = value.astype(BF16)
    low = (value - high.astype(F32)).astype(BF16)
    return jnp.concatenate([high, low, high], axis=axis)


def left(table, value):
    return jnp.dot(table, split3(value, 0), preferred_element_type=F32)


def right(value, table):
    return jnp.dot(split3(value, 1), table, preferred_element_type=F32)


def cube(value):
    return value * value * value


def whole_block(shape):
    return pl.BlockSpec(shape, lambda *_: (0,) * len(shape))


SMEM = pl.BlockSpec(memory_space=pltpu.SMEM)


def call(kernel, name, grid, in_specs, out_specs, out_shape, scratch=(), flops=0, moved=0, aliases=None):
    return pl.pallas_call(
        kernel,
        grid=grid,
        in_specs=in_specs,
        out_specs=out_specs,
        out_shape=out_shape,
        scratch_shapes=list(scratch),
        input_output_aliases=aliases or {},
        compiler_params=pltpu.CompilerParams(vmem_limit_bytes=VMEM_BYTES),
        cost_estimate=pl.CostEstimate(flops=flops, bytes_accessed=moved, transcendentals=0),
        name=name,
    )


def depth_kernel(last_ref, table_ref, initial_ref, end_ref, *out_refs):
    value = jnp.swapaxes(jnp.where(last_ref[0] == 1, initial_ref[...], end_ref[0]), 0, 1)
    rows = jnp.stack([left(table_ref[...], value[row]) for row in range(ROWS)])
    groups, _, _, wide = out_refs[0].shape
    rows = jnp.swapaxes(rows, 0, 1).reshape(groups, -1, ROWS, wide)
    begin = 0
    for out_ref in out_refs:
        planes = out_ref.shape[1]
        out_ref[...] = rows[:, begin:begin + planes]
        begin += planes


def start_kernel(planes, modes_ref, sx_ref, sy_ref, syt_ref, rho_ref, power_ref, right_ref, left_ref, *refs):
    corner_ref, side_ref, high_ref, v_ref, power, to_right_ref, to_left_ref, cubic = refs[-8:]

    @pl.when(pl.program_id(0) == 0)
    def _():
        power[...] = power_ref[...]
        to_right_ref[...] = right_ref[...]
        to_left_ref[...] = left_ref[...]

    groups, _, block, wide = modes_ref.shape
    grid = groups * block
    half = block // 2
    modes = [modes_ref[:, j].reshape(grid, wide) for j in range(planes)]
    along_x = right(jnp.concatenate(modes, axis=0), sx_ref[...])
    terms = [cube(left(sy_ref[...], along_x[j * grid:(j + 1) * grid])) for j in range(planes)]
    along_x = right(jnp.concatenate(terms, axis=0), sx_ref[...])
    for j in range(planes):
        cubic[j] = left(syt_ref[...], along_x[j * grid:(j + 1) * grid])
    for strip in range(2 * groups):
        group, upper = strip // 2, strip % 2
        rows = slice(strip * half, (strip + 1) * half)
        within = slice(upper * half, (upper + 1) * half)
        rho = [rho_ref[node, rows] for node in range(2)]
        carried = [to_left_ref[node, rows] for node in range(2)]
        weight = [power[node, rows] for node in range(2)]
        total = [to_right_ref[node, rows] for node in range(2)]
        for j in reversed(range(planes)):
            mode = modes_ref[group, j, within]
            source = 2.0 * mode - cubic[j, rows]
            if upper:
                high_ref[group, j] = source
            else:
                corner_ref[group, j] = source[:, :wide // 2]
                side_ref[group, j] = source[:, wide // 2:]
            for node, value in enumerate((source, 0.5 * (mode + source))):
                carried[node] = value + rho[node] * carried[node]
                v_ref[node, j, rows] = carried[node]
                v_ref[2 + node, j, rows] = value
                total[node] += weight[node] * value
                weight[node] = weight[node] * rho[node]
        for node in range(2):
            to_left_ref[node, rows] = carried[node]
            power[node, rows] = weight[node]
            to_right_ref[node, rows] = total[node]


def node_kernel(planes, slab, v_ref, from_left_ref, from_right_ref, rho_ref, inverse_ref, kappa_ref,
                sx_ref, sy_ref, sxl_ref, syl_ref, out_ref, left_sum, right_sum, nodes):
    step = pl.program_id(0)
    plane = step * planes

    @pl.when(step == 0)
    def _():
        left_sum[...] = from_left_ref[...]

    @pl.when(plane % ROWS == 0)
    def _():
        rho = rho_ref[...]
        twice = rho * rho
        four = twice * twice
        eight = four * four
        right_sum[...] = lax.fori_loop(
            0, slab // ROWS - plane // ROWS, lambda _, total: total * eight, from_right_ref[...]
        )

    groups, _, half, low = out_ref.shape
    grid = v_ref.shape[2]
    wide = v_ref.shape[3]
    for strip in range(2 * groups):
        rows = slice(strip * half, (strip + 1) * half)
        rho = [rho_ref[node, rows] for node in range(2)]
        inverse = [inverse_ref[node, rows] for node in range(2)]
        kappa = [kappa_ref[node, rows] for node in range(2)]
        before = [left_sum[node, rows] for node in range(2)]
        after = [right_sum[node, rows] for node in range(2)]
        for j in range(planes):
            for node in range(2):
                behind = rho[node] * before[node]
                before[node] = v_ref[2 + node, j, rows] + behind
                nodes[node, j, rows] = kappa[node] * (behind + v_ref[node, j, rows] + after[node])
                after[node] = after[node] * inverse[node]
        for node in range(2):
            left_sum[node, rows] = before[node]
            right_sum[node, rows] = after[node]
    along_x = right(nodes[...].reshape(2 * planes * grid, wide), sx_ref[...])
    fields = [left(sy_ref[...], along_x[j * grid:(j + 1) * grid]) for j in range(2 * planes)]
    terms = [cube(fields[j]) + 4.0 * cube(fields[planes + j]) for j in range(planes)]
    along_x = right(jnp.concatenate(terms, axis=0), sxl_ref[...])
    for j in range(planes):
        term = left(syl_ref[...], along_x[j * grid:(j + 1) * grid])
        out_ref[:, j] = term.reshape(groups, half, low)


def joined(refs):
    parts = [ref[...] for ref in refs]
    parts = jnp.concatenate(parts, axis=1)
    return parts.reshape(parts.shape[0] * parts.shape[1], *parts.shape[2:])


def low_kernel(factor, fine_ref, coarse_ref, table_ref, eigen_ref, coarse_eigen_ref, corner_ref, start_ref,
               out_ref, gathered_ref):
    base = pl.program_id(0) * ROWS
    coarse = start_ref.shape[0]
    sources = jnp.swapaxes(corner_ref[...], 0, 1)
    starts = jnp.swapaxes(start_ref[...], 0, 1)
    ends, gathered = [], []
    for row in range(ROWS):
        source = left(table_ref[...], sources[row])
        eigen = eigen_ref[...] + fine_ref[base + row]
        node_end = source / (1.0 + eigen)
        ends.append(node_end)
        source, node_end, eigen = source[:coarse], node_end[:coarse], eigen[:coarse]
        start = starts[row]
        node_mid = 0.5 * (start + source) / (1.0 + 0.5 * eigen)
        rate = source - (1.0 + eigen) * start + (1.0 - eigen) * (4.0 * node_mid + node_end)
        coarse_eigen = coarse_eigen_ref[...] + coarse_ref[base + row]
        gathered.append(factor * (rate / 6.0 + coarse_eigen * node_end))
    out_ref[...] = jnp.swapaxes(jnp.stack(ends), 0, 1)
    gathered_ref[...] = jnp.swapaxes(jnp.stack(gathered), 0, 1)


def offset_kernel(factor, first_ref, coarse_ref, table_ref, coarse_eigen_ref, gathered_ref, start_ref, cubic_ref,
                  out_ref):
    base = pl.program_id(0) * ROWS
    first = first_ref[0] == 1
    cubics = jnp.swapaxes(cubic_ref[...], 0, 1)
    given = jnp.swapaxes(gathered_ref[...] + jnp.where(first, factor * start_ref[...], 0.0), 0, 1)
    rows = []
    for row in range(ROWS):
        total = given[row] - (factor / 6.0) * left(table_ref[...], cubics[row])
        rows.append(total / (1.0 + coarse_eigen_ref[...] + coarse_ref[base + row]))
    out_ref[...] = jnp.swapaxes(jnp.stack(rows), 0, 1)


def finish_kernel(fine_ref, table_ref, eigen_ref, *refs):
    base = pl.program_id(0) * ROWS
    out_ref = refs[-1]
    sources = jnp.swapaxes(joined(refs[:-2]), 0, 1)
    rows = []
    for row in range(ROWS):
        source = left(table_ref[...], sources[row])
        rows.append(source / (1.0 + eigen_ref[...] + fine_ref[base + row]))
    out_ref[...] = jnp.swapaxes(jnp.stack(rows), 0, 1)


def shifted(value, axis, by):
    length = lax.axis_size(axis)
    pairs = [(i, i + by) for i in range(length) if 0 <= i + by < length]
    return lax.ppermute(value, axis, pairs)


def turned(value, axis):
    length = lax.axis_size(axis)
    return lax.ppermute(value, axis, [(i, (i + 1) % length) for i in range(length)])


def exchange(value):
    return lax.all_to_all(value, "gx", split_axis=0, concat_axis=0, tiled=True)


def after(value, *earlier):
    return lax.optimization_barrier((value, *earlier))


def per_device(end_modes, initial_modes):
    grid = initial_modes.shape[0]
    coarse = grid // 2
    groups = lax.axis_size("gx")
    block = grid // groups
    half = block // 2
    planes = 4
    slice_index = lax.axis_index("tm")
    group_index = lax.axis_index("gx")
    is_first = slice_index == 0
    slices = lax.axis_size("tm")
    first = is_first.astype(jnp.int32)[None]
    last = (slice_index == slices - 1).astype(jnp.int32)[None]
    order = fine_order(grid, groups)
    sine = sine_matrix(grid)
    fine_w, coarse_w = omega(grid), omega(coarse)
    factor = ((coarse + 1) / (grid + 1)) ** 1.5
    unit = grid * block * grid

    flat = fine_w[order][:, None] + fine_w[None, :]
    scale = np.array([1.0, 0.5])[:, None, None] * DIFFUSION
    diagonal = 1.0 / scale + 2.0 + flat[None]
    rho = 2.0 / (diagonal + np.sqrt(diagonal * diagonal - 4.0))
    inverse = 1.0 / rho
    kappa = 1.0 / (scale * (inverse - rho))
    rho, inverse, kappa = (t.astype(np.float32) for t in (rho, inverse, kappa))
    rho_slab = (rho.astype(np.float64) ** block).astype(np.float32)
    rounds = 1
    while np.float32(float(rho.max()) ** (block * rounds)) > 0:
        rounds += 1

    depth_table = left_table(sine)
    x_table = right_table(sine)
    y_table = left_table(sine[:, order])
    back_table = left_table(sine[order, :])
    x_low_table = right_table(sine[:, :coarse])
    low_table = left_table(sine[:coarse, :])
    eigen = (DIFFUSION * (fine_w[:, None] + fine_w[None, :])).astype(np.float32)
    coarse_eigen = (0.25 * DIFFUSION * (coarse_w[:, None] + coarse_w[None, :])).astype(np.float32)
    fine_own = lax.dynamic_slice(jnp.asarray((DIFFUSION * fine_w[order]).astype(np.float32)), (group_index * block,), (block,))
    coarse_own = lax.dynamic_slice(
        jnp.asarray((0.25 * DIFFUSION * coarse_w).astype(np.float32)), (group_index * half,), (half,)
    )

    rows_spec = pl.BlockSpec((grid, ROWS, grid), lambda i: (0, i, 0))
    table_spec = whole_block(depth_table.shape)
    quarter = block // 4
    middle = 3 * quarter // planes // 2 * planes
    lengths = (quarter, middle, block - quarter - middle)
    begins = (0, quarter, quarter + middle)
    parts = len(lengths)
    end_begin = begins[1]

    def depth(chosen):
        span = slice(begins[chosen[0]], begins[chosen[-1]] + lengths[chosen[-1]])
        table = depth_table.reshape(groups, block, -1)[:, span].reshape(-1, depth_table.shape[1])
        return pl.pallas_call(
            depth_kernel,
            grid_spec=pltpu.PrefetchScalarGridSpec(
                num_scalar_prefetch=1,
                grid=(block // ROWS,),
                in_specs=[
                    whole_block(table.shape),
                    pl.BlockSpec((grid, ROWS, grid), lambda i, last: (0, i * last[0], 0)),
                    pl.BlockSpec((1, grid, ROWS, grid), lambda i, last: (0, 0, i * (1 - last[0]), 0)),
                ],
                out_specs=[
                    pl.BlockSpec((groups, lengths[part], ROWS, grid), lambda i, last: (0, 0, i, 0))
                    for part in chosen
                ],
            ),
            out_shape=[jax.ShapeDtypeStruct((groups, lengths[part], block, grid), F32) for part in chosen],
            compiler_params=pltpu.CompilerParams(vmem_limit_bytes=VMEM_BYTES),
            cost_estimate=pl.CostEstimate(flops=6 * unit * grid, bytes_accessed=8 * unit, transcendentals=0),
            name="depth",
        )(last, table, initial_modes, end_modes)

    outgoing = [*depth((0, 1)), *depth((2,))]
    for part in (1, 0):
        outgoing[part] = turned(outgoing[part], "tm")

    pair = (2, grid, grid)
    pair_spec = whole_block(pair)
    whole = (groups, block, half)
    shapes = [
        (*whole, coarse),
        (*whole, coarse),
        (groups, block - end_begin, half, grid),
        (4, block, grid, grid),
    ]
    arrays = None
    state = (np.ones(pair, np.float32), np.zeros(pair, np.float32), np.zeros(pair, np.float32))
    backs, states = {}, {}
    for part in reversed(range(parts)):
        given = outgoing[part]
        if part + 1 in backs:
            given, *_ = after(given, backs[part + 1], *states.get(part + 2, ()))
        backs[part] = exchange(given)
        modes = turned(backs[part], "tm") if part == parts - 1 else backs[part]
        steps = lengths[part] // planes
        bases = [begins[part] // planes] * 4
        if part >= 1:
            bases[2] = (begins[part] - end_begin) // planes
        else:
            shapes[2] = (groups, end_begin, half, grid)
        specs = [
            pl.BlockSpec(
                (4, planes, grid, grid) if n == 3 else (groups, planes, half, shapes[n][3]),
                lambda i, base=base, steps=steps: (0, base + steps - 1 - i, 0, 0),
            )
            for n, base in enumerate(bases)
        ]
        held = [n for n in range(4) if arrays is not None and not (part == 0 and n == 2)]
        outs = call(
            functools.partial(start_kernel, planes),
            "start",
            (steps,),
            [
                pl.BlockSpec((groups, planes, block, grid), lambda i, steps=steps: (0, steps - 1 - i, 0, 0)),
                whole_block(x_table.shape),
                table_spec,
                table_spec,
                pair_spec,
                pair_spec,
                pair_spec,
                pair_spec,
            ] + [pl.BlockSpec(memory_space=pl.ANY)] * len(held),
            specs + [pair_spec] * 3,
            [jax.ShapeDtypeStruct(shape, F32) for shape in shapes] + [jax.ShapeDtypeStruct(pair, F32)] * 3,
            scratch=[pltpu.VMEM((planes, grid, grid), F32)],
            flops=24 * unit * grid * lengths[part] // block,
            moved=24 * unit * lengths[part] // block,
            aliases={8 + place: n for place, n in enumerate(held)},
        )(modes, x_table, y_table, back_table, rho, *state, *(arrays[n] for n in held))
        if part >= 1:
            high_rest = outs[2]
        else:
            high_first = outs[2]
        arrays, state = outs[:4], outs[4:]
        states[part] = state
    corner, side, _, v = arrays
    _, to_right, to_left = state
    high_rest, backs[0] = after(high_rest, backs[0])
    high_rest_back = exchange(high_rest.reshape(-1, half, grid))
    at_start, at_end = group_index == 0, group_index == groups - 1
    if rounds <= 2:
        rightward = jnp.where(at_start, to_right - rho_slab * (rho * to_left), to_right)
        leftward = jnp.where(at_end, to_left - rho_slab * (rho * to_right), to_left)
        from_left = shifted(rightward, "gx", 1) + rho_slab * shifted(rightward, "gx", 2)
        from_right = shifted(leftward, "gx", -1) + rho_slab * shifted(leftward, "gx", -2)
        from_left, from_right = (
            jnp.where(at_start, -rho * (to_left + rho_slab * from_right), from_left),
            jnp.where(at_end, -rho * (to_right + rho_slab * from_left), from_right),
        )
    else:
        from_left = jnp.zeros(pair, F32)
        from_right = jnp.zeros(pair, F32)
        for _ in range(rounds):
            rightward = to_right + rho_slab * from_left
            leftward = to_left + rho_slab * from_right
            from_left = jnp.where(at_start, -rho * leftward, shifted(rightward, "gx", 1))
            from_right = jnp.where(at_end, -rho * rightward, shifted(leftward, "gx", -1))

    corner, high_rest_back, from_left, from_right = after(corner, high_rest_back, from_left, from_right)
    corner_back = exchange(corner.reshape(grid, half, coarse))
    cubic = call(
        functools.partial(node_kernel, planes, block),
        "nodes",
        (block // planes,),
        [pl.BlockSpec((4, planes, grid, grid), lambda i: (0, i, 0, 0))]
        + [pair_spec] * 5
        + [
            whole_block(x_table.shape),
            table_spec,
            whole_block(x_low_table.shape),
            whole_block(low_table.shape),
        ],
        pl.BlockSpec((groups, planes, half, coarse), lambda i: (0, i, 0, 0)),
        jax.ShapeDtypeStruct((groups, block, half, coarse), F32),
        scratch=[pltpu.VMEM(pair, F32), pltpu.VMEM(pair, F32), pltpu.VMEM((2, planes, grid, grid), F32)],
        flops=28 * unit * grid,
        moved=17 * unit,
    )(v, from_left, from_right, rho, inverse, kappa, x_table, y_table, x_low_table, low_table)
    cubic, corner_back = after(cubic, corner_back)
    cubic_back = exchange(cubic.reshape(grid, half, coarse))
    high_first, cubic_back = after(high_first, cubic_back)
    high_first_back = exchange(high_first.reshape(-1, half, grid))
    side, high_first_back = after(side, high_first_back)
    side_back = exchange(side.reshape(grid, half, coarse))
    high_backs = [part.reshape(groups, -1, half, grid) for part in (high_first_back, high_rest_back)]
    start_low = jnp.where(
        is_first, initial_modes[:coarse, :half, :coarse], shifted(end_modes[0, :coarse, :half, :coarse], "tm", 1)
    )

    low_spec = pl.BlockSpec((coarse, ROWS, coarse), lambda i: (0, i, 0))
    coarse_eigen_spec = whole_block(coarse_eigen.shape)
    quarter_spec = pl.BlockSpec((grid, ROWS, coarse), lambda i: (0, i, 0))
    corner_shape = jax.ShapeDtypeStruct((coarse, half, coarse), F32)
    result_shape = jax.ShapeDtypeStruct((grid, block, grid), F32)
    result, gathered = call(
        functools.partial(low_kernel, factor),
        "low",
        (half // ROWS,),
        [SMEM, SMEM, table_spec, whole_block((grid, coarse)), coarse_eigen_spec, quarter_spec, low_spec],
        [quarter_spec, low_spec],
        [result_shape, corner_shape],
        flops=2 * unit * grid,
        moved=3 * unit,
    )(fine_own, coarse_own, depth_table, eigen[:, :coarse], coarse_eigen, corner_back, start_low)
    offset = call(
        functools.partial(offset_kernel, factor),
        "offset",
        (half // ROWS,),
        [SMEM, SMEM, whole_block(low_table.shape), coarse_eigen_spec, low_spec, low_spec, quarter_spec],
        low_spec,
        corner_shape,
        flops=unit * grid,
        moved=2 * unit,
    )(first, coarse_own, low_table, coarse_eigen, gathered, start_low, cubic_back)

    def finish(result, sources, weights, eigen, row, column):
        width = eigen.shape[1]
        return call(
            finish_kernel,
            "finish",
            (half // ROWS,),
            [SMEM, table_spec, whole_block(eigen.shape)]
            + [pl.BlockSpec((groups, part.shape[1], ROWS, width), lambda i: (0, 0, i, 0)) for part in sources]
            + [pl.BlockSpec(memory_space=pl.ANY)],
            pl.BlockSpec((grid, ROWS, width), lambda i: (0, row // ROWS + i, column)),
            result_shape,
            flops=3 * unit * width,
            moved=5 * unit * width // grid,
            aliases={3 + len(sources): 0},
        )(weights, depth_table, eigen, *sources, result)

    result = finish(result, high_backs, fine_own[half:], eigen, half, 0)
    decay = 1.0 / (1.0 + coarse_eigen[:, None, :] + coarse_own[None, :, None])
    coarse_end = offset
    for turn in range(1, slices):
        incoming = lax.ppermute(coarse_end, "tm", [(turn - 1, turn)])
        coarse_end = jnp.where(slice_index == turn, decay * incoming + offset, coarse_end)
    result = result.at[:coarse, :half, :coarse].set(coarse_end / factor)
    result = finish(
        result, [side_back.reshape(groups, block, half, coarse)], fine_own[:half], eigen[:, coarse:], 0, 1
    )
    return (result[None], coarse_end[None])


def solution(mesh):
    return jax.shard_map(
        per_device,
        mesh=mesh,
        in_specs=(P("tm", None, "gx", None), P(None, "gx", None)),
        out_specs=(P("tm", None, "gx", None), P("tm", None, "gx", None)),
        check_vma=False,
    )
```

```python
import functools
import math

import jax
import jax.numpy as jnp
import ml_dtypes
import numpy as np
from jax import lax
from jax.experimental import pallas as pl
from jax.experimental.pallas import tpu as pltpu
from jax.sharding import PartitionSpec as P

DIFFUSION = 0.25
BF16 = jnp.bfloat16
F32 = jnp.float32
ROWS = 8
VMEM_BYTES = 56 * 1024 * 1024


def sine_matrix(length):
    index = np.arange(1, length + 1)
    phase = np.outer(index, index) % (2 * (length + 1))
    return np.sin(phase * (math.pi / (length + 1))) * math.sqrt(2.0 / (length + 1))


def omega(count):
    return 2.0 - 2.0 * np.cos((np.arange(count) + 1.0) * (math.pi / (count + 1)))


def fine_order(grid, groups):
    block, coarse = grid // groups, grid // 2
    half = block // 2
    position = np.arange(grid)
    within, group = position % block, position // block
    return np.where(within < half, group * half + within, coarse + group * half + within - half)


def halves(table):
    high = table.astype(ml_dtypes.bfloat16)
    low = (table - high.astype(np.float64)).astype(ml_dtypes.bfloat16)
    return high, low


def left_table(table):
    high, low = halves(table)
    return np.concatenate([high, high, low], axis=1)


def right_table(table):
    high, low = halves(table)
    return np.concatenate([high, high, low], axis=0)


def split3(value, axis):
    high = value.astype(BF16)
    low = (value - high.astype(F32)).astype(BF16)
    return jnp.concatenate([high, low, high], axis=axis)


def left(table, value):
    return jnp.dot(table, split3(value, 0), preferred_element_type=F32)


def right(value, table):
    return jnp.dot(split3(value, 1), table, preferred_element_type=F32)


def cube(value):
    return value * value * value


def whole_block(shape):
    return pl.BlockSpec(shape, lambda *_: (0,) * len(shape))


SMEM = pl.BlockSpec(memory_space=pltpu.SMEM)


def call(kernel, name, grid, in_specs, out_specs, out_shape, scratch=(), flops=0, moved=0, aliases=None):
    return pl.pallas_call(
        kernel,
        grid=grid,
        in_specs=in_specs,
        out_specs=out_specs,
        out_shape=out_shape,
        scratch_shapes=list(scratch),
        input_output_aliases=aliases or {},
        compiler_params=pltpu.CompilerParams(vmem_limit_bytes=VMEM_BYTES),
        cost_estimate=pl.CostEstimate(flops=flops, bytes_accessed=moved, transcendentals=0),
        name=name,
    )


def depth_kernel(last_ref, table_ref, initial_ref, end_ref, *out_refs):
    value = jnp.swapaxes(jnp.where(last_ref[0] == 1, initial_ref[...], end_ref[0]), 0, 1)
    rows = jnp.stack([left(table_ref[...], value[row]) for row in range(ROWS)])
    groups, _, _, wide = out_refs[0].shape
    rows = jnp.swapaxes(rows, 0, 1).reshape(groups, -1, ROWS, wide)
    begin = 0
    for out_ref in out_refs:
        planes = out_ref.shape[1]
        out_ref[...] = rows[:, begin:begin + planes]
        begin += planes


def start_kernel(planes, modes_ref, sx_ref, sy_ref, syt_ref, rho_ref, power_ref, right_ref, left_ref, *refs):
    corner_ref, rest_ref, v_ref, power, to_right_ref, to_left_ref, cubic = refs[-7:]

    @pl.when(pl.program_id(0) == 0)
    def _():
        power[...] = power_ref[...]
        to_right_ref[...] = right_ref[...]
        to_left_ref[...] = left_ref[...]

    groups, _, block, wide = modes_ref.shape
    grid = groups * block
    half = block // 2
    modes = [modes_ref[:, j].reshape(grid, wide) for j in range(planes)]
    along_x = right(jnp.concatenate(modes, axis=0), sx_ref[...])
    terms = [cube(left(sy_ref[...], along_x[j * grid:(j + 1) * grid])) for j in range(planes)]
    along_x = right(jnp.concatenate(terms, axis=0), sx_ref[...])
    for j in range(planes):
        cubic[j] = left(syt_ref[...], along_x[j * grid:(j + 1) * grid])
    for strip in range(2 * groups):
        group, upper = strip // 2, strip % 2
        rows = slice(strip * half, (strip + 1) * half)
        within = slice(upper * half, (upper + 1) * half)
        rho = [rho_ref[node, rows] for node in range(2)]
        carried = [to_left_ref[node, rows] for node in range(2)]
        weight = [power[node, rows] for node in range(2)]
        total = [to_right_ref[node, rows] for node in range(2)]
        for j in reversed(range(planes)):
            mode = modes_ref[group, j, within]
            source = 2.0 * mode - cubic[j, rows]
            if upper:
                rest_ref[group, j, :, :wide] = source
            else:
                corner_ref[group, j] = source[:, :wide // 2]
                rest_ref[group, j, :, wide:] = source[:, wide // 2:]
            for node, value in enumerate((source, 0.5 * (mode + source))):
                carried[node] = value + rho[node] * carried[node]
                v_ref[node, j, rows] = carried[node]
                v_ref[2 + node, j, rows] = value
                total[node] += weight[node] * value
                weight[node] = weight[node] * rho[node]
        for node in range(2):
            to_left_ref[node, rows] = carried[node]
            power[node, rows] = weight[node]
            to_right_ref[node, rows] = total[node]


def node_kernel(planes, slab, v_ref, from_left_ref, from_right_ref, rho_ref, inverse_ref, kappa_ref,
                sx_ref, sy_ref, sxl_ref, syl_ref, out_ref, left_sum, right_sum, nodes):
    step = pl.program_id(0)
    plane = step * planes

    @pl.when(step == 0)
    def _():
        left_sum[...] = from_left_ref[...]

    @pl.when(plane % ROWS == 0)
    def _():
        rho = rho_ref[...]
        twice = rho * rho
        four = twice * twice
        eight = four * four
        right_sum[...] = lax.fori_loop(
            0, slab // ROWS - plane // ROWS, lambda _, total: total * eight, from_right_ref[...]
        )

    groups, _, half, low = out_ref.shape
    grid = v_ref.shape[2]
    wide = v_ref.shape[3]
    for strip in range(2 * groups):
        rows = slice(strip * half, (strip + 1) * half)
        rho = [rho_ref[node, rows] for node in range(2)]
        inverse = [inverse_ref[node, rows] for node in range(2)]
        kappa = [kappa_ref[node, rows] for node in range(2)]
        before = [left_sum[node, rows] for node in range(2)]
        after = [right_sum[node, rows] for node in range(2)]
        for j in range(planes):
            for node in range(2):
                behind = rho[node] * before[node]
                before[node] = v_ref[2 + node, j, rows] + behind
                nodes[node, j, rows] = kappa[node] * (behind + v_ref[node, j, rows] + after[node])
                after[node] = after[node] * inverse[node]
        for node in range(2):
            left_sum[node, rows] = before[node]
            right_sum[node, rows] = after[node]
    along_x = right(nodes[...].reshape(2 * planes * grid, wide), sx_ref[...])
    fields = [left(sy_ref[...], along_x[j * grid:(j + 1) * grid]) for j in range(2 * planes)]
    terms = [cube(fields[j]) + 4.0 * cube(fields[planes + j]) for j in range(planes)]
    along_x = right(jnp.concatenate(terms, axis=0), sxl_ref[...])
    for j in range(planes):
        term = left(syl_ref[...], along_x[j * grid:(j + 1) * grid])
        out_ref[:, j] = term.reshape(groups, half, low)


def joined(refs):
    parts = jnp.concatenate([ref[...] for ref in refs], axis=1)
    return parts.reshape(parts.shape[0] * parts.shape[1], *parts.shape[2:])


def low_kernel(factor, fine_ref, coarse_ref, table_ref, eigen_ref, coarse_eigen_ref, corner_ref, start_ref,
               out_ref, gathered_ref):
    base = pl.program_id(0) * ROWS
    coarse = start_ref.shape[0]
    sources = jnp.swapaxes(corner_ref[...], 0, 1)
    starts = jnp.swapaxes(start_ref[...], 0, 1)
    ends, gathered = [], []
    for row in range(ROWS):
        source = left(table_ref[...], sources[row])
        eigen = eigen_ref[...] + fine_ref[base + row]
        node_end = source / (1.0 + eigen)
        ends.append(node_end[coarse:])
        source, node_end, eigen = source[:coarse], node_end[:coarse], eigen[:coarse]
        start = starts[row]
        node_mid = 0.5 * (start + source) / (1.0 + 0.5 * eigen)
        rate = source - (1.0 + eigen) * start + (1.0 - eigen) * (4.0 * node_mid + node_end)
        coarse_eigen = coarse_eigen_ref[...] + coarse_ref[base + row]
        gathered.append(factor * (rate / 6.0 + coarse_eigen * node_end))
    out_ref[...] = jnp.swapaxes(jnp.stack(ends), 0, 1)
    gathered_ref[...] = jnp.swapaxes(jnp.stack(gathered), 0, 1)


def offset_kernel(factor, first_ref, coarse_ref, table_ref, coarse_eigen_ref, gathered_ref, start_ref, cubic_ref,
                  out_ref):
    base = pl.program_id(0) * ROWS
    first = first_ref[0] == 1
    cubics = jnp.swapaxes(cubic_ref[...], 0, 1)
    given = jnp.swapaxes(gathered_ref[...] + jnp.where(first, factor * start_ref[...], 0.0), 0, 1)
    rows = []
    for row in range(ROWS):
        total = given[row] - (factor / 6.0) * left(table_ref[...], cubics[row])
        rows.append(total / (1.0 + coarse_eigen_ref[...] + coarse_ref[base + row]))
    out_ref[...] = jnp.swapaxes(jnp.stack(rows), 0, 1)


def finish_kernel(factor, fine_ref, table_ref, eigen_ref, corner_ref, end_ref, *refs):
    out_ref = refs[-1]
    coarse = end_ref.shape[0]
    steps = pl.num_programs(0) // 2
    step = pl.program_id(0)
    base = (step + steps) % (2 * steps) * ROWS
    fields = [joined(refs[n:n + 2]) for n in range(0, 6, 2)]

    def solved(source, eigen):
        source = jnp.swapaxes(source, 0, 1)
        rows = [left(table_ref[...], source[row]) / (1.0 + eigen + fine_ref[base + row]) for row in range(ROWS)]
        return jnp.swapaxes(jnp.stack(rows), 0, 1)

    @pl.when(step < steps)
    def _():
        out_ref[...] = solved(jnp.concatenate(fields[:2], axis=2), eigen_ref[...])

    @pl.when(step >= steps)
    def _():
        out_ref[:coarse, :, :coarse] = end_ref[...] / factor
        out_ref[coarse:, :, :coarse] = corner_ref[...]
        out_ref[:, :, coarse:] = solved(fields[2], eigen_ref[:, coarse:])


def shifted(value, axis, by):
    length = lax.axis_size(axis)
    pairs = [(i, i + by) for i in range(length) if 0 <= i + by < length]
    return lax.ppermute(value, axis, pairs)


def turned(value, axis):
    length = lax.axis_size(axis)
    return lax.ppermute(value, axis, [(i, (i + 1) % length) for i in range(length)])


def exchange(value):
    return lax.all_to_all(value, "gx", split_axis=0, concat_axis=0, tiled=True)


def after(value, *earlier):
    return lax.optimization_barrier((value, *earlier))


def per_device(end_modes, initial_modes):
    grid = initial_modes.shape[0]
    coarse = grid // 2
    groups = lax.axis_size("gx")
    block = grid // groups
    half = block // 2
    planes = 4
    slice_index = lax.axis_index("tm")
    group_index = lax.axis_index("gx")
    is_first = slice_index == 0
    slices = lax.axis_size("tm")
    first = is_first.astype(jnp.int32)[None]
    last = (slice_index == slices - 1).astype(jnp.int32)[None]
    order = fine_order(grid, groups)
    sine = sine_matrix(grid)
    fine_w, coarse_w = omega(grid), omega(coarse)
    factor = ((coarse + 1) / (grid + 1)) ** 1.5
    unit = grid * block * grid

    flat = fine_w[order][:, None] + fine_w[None, :]
    scale = np.array([1.0, 0.5])[:, None, None] * DIFFUSION
    diagonal = 1.0 / scale + 2.0 + flat[None]
    rho = 2.0 / (diagonal + np.sqrt(diagonal * diagonal - 4.0))
    inverse = 1.0 / rho
    kappa = 1.0 / (scale * (inverse - rho))
    rho, inverse, kappa = (t.astype(np.float32) for t in (rho, inverse, kappa))
    rho_slab = (rho.astype(np.float64) ** block).astype(np.float32)
    rounds = 1
    while np.float32(float(rho.max()) ** (block * rounds)) > 0:
        rounds += 1

    depth_table = left_table(sine)
    x_table = right_table(sine)
    y_table = left_table(sine[:, order])
    back_table = left_table(sine[order, :])
    x_low_table = right_table(sine[:, :coarse])
    low_table = left_table(sine[:coarse, :])
    eigen = (DIFFUSION * (fine_w[:, None] + fine_w[None, :])).astype(np.float32)
    coarse_eigen = (0.25 * DIFFUSION * (coarse_w[:, None] + coarse_w[None, :])).astype(np.float32)
    fine_own = lax.dynamic_slice(jnp.asarray((DIFFUSION * fine_w[order]).astype(np.float32)), (group_index * block,), (block,))
    coarse_own = lax.dynamic_slice(
        jnp.asarray((0.25 * DIFFUSION * coarse_w).astype(np.float32)), (group_index * half,), (half,)
    )

    rows_spec = pl.BlockSpec((grid, ROWS, grid), lambda i: (0, i, 0))
    table_spec = whole_block(depth_table.shape)
    lengths = (block // 2, block - block // 2)
    begins = (0, block // 2)
    parts = len(lengths)
    end_begin = begins[1]

    def depth(chosen):
        span = slice(begins[chosen[0]], begins[chosen[-1]] + lengths[chosen[-1]])
        table = depth_table.reshape(groups, block, -1)[:, span].reshape(-1, depth_table.shape[1])
        return pl.pallas_call(
            depth_kernel,
            grid_spec=pltpu.PrefetchScalarGridSpec(
                num_scalar_prefetch=1,
                grid=(block // ROWS,),
                in_specs=[
                    whole_block(table.shape),
                    pl.BlockSpec((grid, ROWS, grid), lambda i, last: (0, i * last[0], 0)),
                    pl.BlockSpec((1, grid, ROWS, grid), lambda i, last: (0, 0, i * (1 - last[0]), 0)),
                ],
                out_specs=[
                    pl.BlockSpec((groups, lengths[part], ROWS, grid), lambda i, last: (0, 0, i, 0))
                    for part in chosen
                ],
            ),
            out_shape=[jax.ShapeDtypeStruct((groups, lengths[part], block, grid), F32) for part in chosen],
            compiler_params=pltpu.CompilerParams(vmem_limit_bytes=VMEM_BYTES),
            cost_estimate=pl.CostEstimate(flops=6 * unit * grid, bytes_accessed=8 * unit, transcendentals=0),
            name="depth",
        )(last, table, initial_modes, end_modes)

    outgoing = [*depth((0,)), *depth((1,))]
    outgoing[0] = turned(outgoing[0], "tm")

    pair = (2, grid, grid)
    pair_spec = whole_block(pair)
    whole = (groups, block, half)
    shapes = [
        (*whole, coarse),
        (groups, block - end_begin, half, grid + coarse),
        (4, block, grid, grid),
    ]
    arrays = None
    state = (np.ones(pair, np.float32), np.zeros(pair, np.float32), np.zeros(pair, np.float32))
    backs, states = {}, {}
    for part in reversed(range(parts)):
        given = outgoing[part]
        if part + 1 in backs:
            given, *_ = after(given, backs[part + 1], *states.get(part + 2, ()))
        backs[part] = exchange(given)
        modes = turned(backs[part], "tm") if part == parts - 1 else backs[part]
        steps = lengths[part] // planes
        bases = [begins[part] // planes] * 3
        if part >= 1:
            bases[1] = (begins[part] - end_begin) // planes
        else:
            shapes[1] = (groups, end_begin, half, grid + coarse)
        specs = [
            pl.BlockSpec(
                (4, planes, grid, grid) if n == 2 else (groups, planes, half, shapes[n][3]),
                lambda i, base=base, steps=steps: (0, base + steps - 1 - i, 0, 0),
            )
            for n, base in enumerate(bases)
        ]
        held = [n for n in range(3) if arrays is not None and not (part == 0 and n == 1)]
        outs = call(
            functools.partial(start_kernel, planes),
            "start",
            (steps,),
            [
                pl.BlockSpec((groups, planes, block, grid), lambda i, steps=steps: (0, steps - 1 - i, 0, 0)),
                whole_block(x_table.shape),
                table_spec,
                table_spec,
                pair_spec,
                pair_spec,
                pair_spec,
                pair_spec,
            ] + [pl.BlockSpec(memory_space=pl.ANY)] * len(held),
            specs + [pair_spec] * 3,
            [jax.ShapeDtypeStruct(shape, F32) for shape in shapes] + [jax.ShapeDtypeStruct(pair, F32)] * 3,
            scratch=[pltpu.VMEM((planes, grid, grid), F32)],
            flops=24 * unit * grid * lengths[part] // block,
            moved=24 * unit * lengths[part] // block,
            aliases={8 + place: n for place, n in enumerate(held)},
        )(modes, x_table, y_table, back_table, rho, *state, *(arrays[n] for n in held))
        if part >= 1:
            rest_last = outs[1]
        else:
            rest_first = outs[1]
        arrays, state = outs[:3], outs[3:]
        states[part] = state
    corner, _, v = arrays
    _, to_right, to_left = state
    rest_last, backs[0] = after(rest_last, backs[0])
    rest_last_back = exchange(rest_last)
    at_start, at_end = group_index == 0, group_index == groups - 1
    if rounds <= 2:
        rightward = jnp.where(at_start, to_right - rho_slab * (rho * to_left), to_right)
        leftward = jnp.where(at_end, to_left - rho_slab * (rho * to_right), to_left)
        from_left = shifted(rightward, "gx", 1) + rho_slab * shifted(rightward, "gx", 2)
        from_right = shifted(leftward, "gx", -1) + rho_slab * shifted(leftward, "gx", -2)
        from_left, from_right = (
            jnp.where(at_start, -rho * (to_left + rho_slab * from_right), from_left),
            jnp.where(at_end, -rho * (to_right + rho_slab * from_left), from_right),
        )
    else:
        from_left = jnp.zeros(pair, F32)
        from_right = jnp.zeros(pair, F32)
        for _ in range(rounds):
            rightward = to_right + rho_slab * from_left
            leftward = to_left + rho_slab * from_right
            from_left = jnp.where(at_start, -rho * leftward, shifted(rightward, "gx", 1))
            from_right = jnp.where(at_end, -rho * rightward, shifted(leftward, "gx", -1))

    corner, rest_last_back, from_left, from_right = after(corner, rest_last_back, from_left, from_right)
    corner_back = exchange(corner.reshape(grid, half, coarse))
    cubic = call(
        functools.partial(node_kernel, planes, block),
        "nodes",
        (block // planes,),
        [pl.BlockSpec((4, planes, grid, grid), lambda i: (0, i, 0, 0))]
        + [pair_spec] * 5
        + [
            whole_block(x_table.shape),
            table_spec,
            whole_block(x_low_table.shape),
            whole_block(low_table.shape),
        ],
        pl.BlockSpec((groups, planes, half, coarse), lambda i: (0, i, 0, 0)),
        jax.ShapeDtypeStruct((groups, block, half, coarse), F32),
        scratch=[pltpu.VMEM(pair, F32), pltpu.VMEM(pair, F32), pltpu.VMEM((2, planes, grid, grid), F32)],
        flops=28 * unit * grid,
        moved=17 * unit,
    )(v, from_left, from_right, rho, inverse, kappa, x_table, y_table, x_low_table, low_table)
    cubic, corner_back = after(cubic, corner_back)
    cubic_back = exchange(cubic.reshape(grid, half, coarse))
    rest_first, cubic_back = after(rest_first, cubic_back)
    rest_backs = [exchange(rest_first), rest_last_back]
    start_low = jnp.where(
        is_first, initial_modes[:coarse, :half, :coarse], shifted(end_modes[0, :coarse, :half, :coarse], "tm", 1)
    )

    low_spec = pl.BlockSpec((coarse, ROWS, coarse), lambda i: (0, i, 0))
    coarse_eigen_spec = whole_block(coarse_eigen.shape)
    quarter_spec = pl.BlockSpec((grid, ROWS, coarse), lambda i: (0, i, 0))
    corner_shape = jax.ShapeDtypeStruct((coarse, half, coarse), F32)
    result_shape = jax.ShapeDtypeStruct((grid, block, grid), F32)
    corner_end, gathered = call(
        functools.partial(low_kernel, factor),
        "low",
        (half // ROWS,),
        [SMEM, SMEM, table_spec, whole_block((grid, coarse)), coarse_eigen_spec, quarter_spec, low_spec],
        [low_spec, low_spec],
        [corner_shape, corner_shape],
        flops=2 * unit * grid,
        moved=3 * unit,
    )(fine_own, coarse_own, depth_table, eigen[:, :coarse], coarse_eigen, corner_back, start_low)
    offset = call(
        functools.partial(offset_kernel, factor),
        "offset",
        (half // ROWS,),
        [SMEM, SMEM, whole_block(low_table.shape), coarse_eigen_spec, low_spec, low_spec, quarter_spec],
        low_spec,
        corner_shape,
        flops=unit * grid,
        moved=2 * unit,
    )(first, coarse_own, low_table, coarse_eigen, gathered, start_low, cubic_back)

    decay = 1.0 / (1.0 + coarse_eigen[:, None, :] + coarse_own[None, :, None])
    coarse_end = offset
    for turn in range(1, slices):
        incoming = lax.ppermute(coarse_end, "tm", [(turn - 1, turn)])
        coarse_end = jnp.where(slice_index == turn, decay * incoming + offset, coarse_end)
    turns = half // ROWS
    upper = [
        pl.BlockSpec((groups, part.shape[1], ROWS, coarse), lambda i, n=n: (0, 0, jnp.minimum(i, turns - 1), n))
        for n in range(2)
        for part in rest_backs
    ]
    side = [
        pl.BlockSpec((groups, part.shape[1], ROWS, coarse), lambda i: (0, 0, jnp.maximum(i - turns, 0), 2))
        for part in rest_backs
    ]
    corner_spec = pl.BlockSpec((coarse, ROWS, coarse), lambda i: (0, jnp.maximum(i - turns, 0), 0))
    result = call(
        functools.partial(finish_kernel, factor),
        "finish",
        (2 * turns,),
        [SMEM, table_spec, whole_block(eigen.shape), corner_spec, corner_spec] + upper + side,
        pl.BlockSpec((grid, ROWS, grid), lambda i: (0, (i + turns) % (2 * turns), 0)),
        result_shape,
        flops=5 * unit * grid,
        moved=9 * unit,
    )(fine_own, depth_table, eigen, corner_end, coarse_end, *(rest_backs * 3))
    return (result[None], coarse_end[None])


def solution(mesh):
    return jax.shard_map(
        per_device,
        mesh=mesh,
        in_specs=(P("tm", None, "gx", None), P(None, "gx", None)),
        out_specs=(P("tm", None, "gx", None), P("tm", None, "gx", None)),
        check_vma=False,
    )
```

```python
import functools
import math

import jax
import jax.numpy as jnp
import ml_dtypes
import numpy as np
from jax import lax
from jax.experimental import pallas as pl
from jax.experimental.pallas import tpu as pltpu
from jax.sharding import PartitionSpec as P

DIFFUSION = 0.25
BF16 = jnp.bfloat16
F32 = jnp.float32
ROWS = 8
VMEM_BYTES = 56 * 1024 * 1024


def sine_matrix(length):
    index = np.arange(1, length + 1)
    phase = np.outer(index, index) % (2 * (length + 1))
    return np.sin(phase * (math.pi / (length + 1))) * math.sqrt(2.0 / (length + 1))


def omega(count):
    return 2.0 - 2.0 * np.cos((np.arange(count) + 1.0) * (math.pi / (count + 1)))


def fine_order(grid, groups):
    block, coarse = grid // groups, grid // 2
    half = block // 2
    position = np.arange(grid)
    within, group = position % block, position // block
    return np.where(within < half, group * half + within, coarse + group * half + within - half)


def halves(table):
    high = table.astype(ml_dtypes.bfloat16)
    low = (table - high.astype(np.float64)).astype(ml_dtypes.bfloat16)
    return high, low


def left_table(table):
    high, low = halves(table)
    return np.concatenate([high, high, low], axis=1)


def right_table(table):
    high, low = halves(table)
    return np.concatenate([high, high, low], axis=0)


def split3(value, axis):
    high = value.astype(BF16)
    low = (value - high.astype(F32)).astype(BF16)
    return jnp.concatenate([high, low, high], axis=axis)


def left(table, value):
    return jnp.dot(table, split3(value, 0), preferred_element_type=F32)


def right(value, table):
    return jnp.dot(split3(value, 1), table, preferred_element_type=F32)


def cube(value):
    return value * value * value


def whole_block(shape):
    return pl.BlockSpec(shape, lambda *_: (0,) * len(shape))


SMEM = pl.BlockSpec(memory_space=pltpu.SMEM)


def call(kernel, name, grid, in_specs, out_specs, out_shape, scratch=(), flops=0, moved=0, aliases=None):
    return pl.pallas_call(
        kernel,
        grid=grid,
        in_specs=in_specs,
        out_specs=out_specs,
        out_shape=out_shape,
        scratch_shapes=list(scratch),
        input_output_aliases=aliases or {},
        compiler_params=pltpu.CompilerParams(vmem_limit_bytes=VMEM_BYTES),
        cost_estimate=pl.CostEstimate(flops=flops, bytes_accessed=moved, transcendentals=0),
        name=name,
    )


def depth_kernel(last_ref, table_ref, initial_ref, end_ref, *out_refs):
    value = jnp.swapaxes(jnp.where(last_ref[0] == 1, initial_ref[...], end_ref[0]), 0, 1)
    rows = jnp.stack([left(table_ref[...], value[row]) for row in range(ROWS)])
    groups, _, _, wide = out_refs[0].shape
    rows = jnp.swapaxes(rows, 0, 1).reshape(groups, -1, ROWS, wide)
    begin = 0
    for out_ref in out_refs:
        planes = out_ref.shape[1]
        out_ref[...] = rows[:, begin:begin + planes]
        begin += planes


def start_kernel(planes, modes_ref, sx_ref, sy_ref, syt_ref, rho_ref, power_ref, right_ref, left_ref, *refs):
    corner_ref, rest_ref, v_ref, power, to_right_ref, to_left_ref, cubic = refs[-7:]

    @pl.when(pl.program_id(0) == 0)
    def _():
        power[...] = power_ref[...]
        to_right_ref[...] = right_ref[...]
        to_left_ref[...] = left_ref[...]

    groups, _, block, wide = modes_ref.shape
    grid = groups * block
    half = block // 2
    modes = [modes_ref[:, j].reshape(grid, wide) for j in range(planes)]
    along_x = right(jnp.concatenate(modes, axis=0), sx_ref[...])
    terms = [cube(left(sy_ref[...], along_x[j * grid:(j + 1) * grid])) for j in range(planes)]
    along_x = right(jnp.concatenate(terms, axis=0), sx_ref[...])
    for j in range(planes):
        cubic[j] = left(syt_ref[...], along_x[j * grid:(j + 1) * grid])
    for strip in range(2 * groups):
        group, upper = strip // 2, strip % 2
        rows = slice(strip * half, (strip + 1) * half)
        within = slice(upper * half, (upper + 1) * half)
        rho = [rho_ref[node, rows] for node in range(2)]
        carried = [to_left_ref[node, rows] for node in range(2)]
        weight = [power[node, rows] for node in range(2)]
        total = [to_right_ref[node, rows] for node in range(2)]
        for j in reversed(range(planes)):
            mode = modes_ref[group, j, within]
            source = 2.0 * mode - cubic[j, rows]
            if upper:
                rest_ref[group, j, :, :wide] = source
            else:
                corner_ref[group, j] = source[:, :wide // 2]
                rest_ref[group, j, :, wide:] = source[:, wide // 2:]
            for node, value in enumerate((source, 0.5 * (mode + source))):
                carried[node] = value + rho[node] * carried[node]
                v_ref[node, j, rows] = carried[node]
                v_ref[2 + node, j, rows] = value
                total[node] += weight[node] * value
                weight[node] = weight[node] * rho[node]
        for node in range(2):
            to_left_ref[node, rows] = carried[node]
            power[node, rows] = weight[node]
            to_right_ref[node, rows] = total[node]


def node_kernel(planes, slab, v_ref, from_left_ref, from_right_ref, rho_ref, inverse_ref, kappa_ref,
                sx_ref, sy_ref, sxl_ref, syl_ref, out_ref, left_sum, right_sum, nodes):
    step = pl.program_id(0)
    plane = step * planes

    @pl.when(step == 0)
    def _():
        left_sum[...] = from_left_ref[...]

    @pl.when(plane % ROWS == 0)
    def _():
        rho = rho_ref[...]
        twice = rho * rho
        four = twice * twice
        eight = four * four
        right_sum[...] = lax.fori_loop(
            0, slab // ROWS - plane // ROWS, lambda _, total: total * eight, from_right_ref[...]
        )

    groups, _, half, low = out_ref.shape
    grid = v_ref.shape[2]
    wide = v_ref.shape[3]
    for strip in range(2 * groups):
        rows = slice(strip * half, (strip + 1) * half)
        rho = [rho_ref[node, rows] for node in range(2)]
        inverse = [inverse_ref[node, rows] for node in range(2)]
        kappa = [kappa_ref[node, rows] for node in range(2)]
        before = [left_sum[node, rows] for node in range(2)]
        after = [right_sum[node, rows] for node in range(2)]
        for j in range(planes):
            for node in range(2):
                behind = rho[node] * before[node]
                before[node] = v_ref[2 + node, j, rows] + behind
                nodes[node, j, rows] = kappa[node] * (behind + v_ref[node, j, rows] + after[node])
                after[node] = after[node] * inverse[node]
        for node in range(2):
            left_sum[node, rows] = before[node]
            right_sum[node, rows] = after[node]
    along_x = right(nodes[...].reshape(2 * planes * grid, wide), sx_ref[...])
    fields = [left(sy_ref[...], along_x[j * grid:(j + 1) * grid]) for j in range(2 * planes)]
    terms = [cube(fields[j]) + 4.0 * cube(fields[planes + j]) for j in range(planes)]
    along_x = right(jnp.concatenate(terms, axis=0), sxl_ref[...])
    for j in range(planes):
        term = left(syl_ref[...], along_x[j * grid:(j + 1) * grid])
        out_ref[:, j] = term.reshape(groups, half, low)


def joined(refs):
    parts = jnp.concatenate([ref[...] for ref in refs], axis=1)
    return parts.reshape(parts.shape[0] * parts.shape[1], *parts.shape[2:])


def low_kernel(factor, fine_ref, coarse_ref, table_ref, eigen_ref, coarse_eigen_ref, corner_ref, start_ref,
               out_ref, gathered_ref):
    base = pl.program_id(0) * ROWS
    coarse = start_ref.shape[0]
    sources = jnp.swapaxes(corner_ref[...], 0, 1)
    starts = jnp.swapaxes(start_ref[...], 0, 1)
    ends, gathered = [], []
    for row in range(ROWS):
        source = left(table_ref[...], sources[row])
        eigen = eigen_ref[...] + fine_ref[base + row]
        node_end = source / (1.0 + eigen)
        ends.append(node_end[coarse:])
        source, node_end, eigen = source[:coarse], node_end[:coarse], eigen[:coarse]
        start = starts[row]
        node_mid = 0.5 * (start + source) / (1.0 + 0.5 * eigen)
        rate = source - (1.0 + eigen) * start + (1.0 - eigen) * (4.0 * node_mid + node_end)
        coarse_eigen = coarse_eigen_ref[...] + coarse_ref[base + row]
        gathered.append(factor * (rate / 6.0 + coarse_eigen * node_end))
    out_ref[...] = jnp.swapaxes(jnp.stack(ends), 0, 1)
    gathered_ref[...] = jnp.swapaxes(jnp.stack(gathered), 0, 1)


def offset_kernel(factor, first_ref, coarse_ref, table_ref, coarse_eigen_ref, gathered_ref, start_ref, cubic_ref,
                  out_ref):
    base = pl.program_id(0) * ROWS
    first = first_ref[0] == 1
    cubics = jnp.swapaxes(cubic_ref[...], 0, 1)
    given = jnp.swapaxes(gathered_ref[...] + jnp.where(first, factor * start_ref[...], 0.0), 0, 1)
    rows = []
    for row in range(ROWS):
        total = given[row] - (factor / 6.0) * left(table_ref[...], cubics[row])
        rows.append(total / (1.0 + coarse_eigen_ref[...] + coarse_ref[base + row]))
    out_ref[...] = jnp.swapaxes(jnp.stack(rows), 0, 1)


def finish_kernel(factor, fine_ref, table_ref, eigen_ref, corner_ref, end_ref, *refs):
    out_ref = refs[-1]
    coarse = end_ref.shape[0]
    steps = pl.num_programs(0) // 2
    step = pl.program_id(0)
    base = (step + steps) % (2 * steps) * ROWS
    fields = [joined(refs[n:n + 2]) for n in range(0, 6, 2)]

    def solved(source, eigen):
        source = jnp.swapaxes(source, 0, 1)
        rows = [left(table_ref[...], source[row]) / (1.0 + eigen + fine_ref[base + row]) for row in range(ROWS)]
        return jnp.swapaxes(jnp.stack(rows), 0, 1)

    @pl.when(step < steps)
    def _():
        out_ref[...] = solved(jnp.concatenate(fields[:2], axis=2), eigen_ref[...])

    @pl.when(step >= steps)
    def _():
        out_ref[:coarse, :, :coarse] = end_ref[...] / factor
        out_ref[coarse:, :, :coarse] = corner_ref[...]
        out_ref[:, :, coarse:] = solved(fields[2], eigen_ref[:, coarse:])


def shifted(value, axis, by):
    length = lax.axis_size(axis)
    pairs = [(i, i + by) for i in range(length) if 0 <= i + by < length]
    return lax.ppermute(value, axis, pairs)


def turned(value, axis):
    length = lax.axis_size(axis)
    return lax.ppermute(value, axis, [(i, (i + 1) % length) for i in range(length)])


def exchange(value):
    return lax.all_to_all(value, "gx", split_axis=0, concat_axis=0, tiled=True)


def after(value, *earlier):
    return lax.optimization_barrier((value, *earlier))


def per_device(end_modes, initial_modes):
    grid = initial_modes.shape[0]
    coarse = grid // 2
    groups = lax.axis_size("gx")
    block = grid // groups
    half = block // 2
    planes = 4
    slice_index = lax.axis_index("tm")
    group_index = lax.axis_index("gx")
    is_first = slice_index == 0
    slices = lax.axis_size("tm")
    first = is_first.astype(jnp.int32)[None]
    last = (slice_index == slices - 1).astype(jnp.int32)[None]
    order = fine_order(grid, groups)
    sine = sine_matrix(grid)
    fine_w, coarse_w = omega(grid), omega(coarse)
    factor = ((coarse + 1) / (grid + 1)) ** 1.5
    unit = grid * block * grid

    flat = fine_w[order][:, None] + fine_w[None, :]
    scale = np.array([1.0, 0.5])[:, None, None] * DIFFUSION
    diagonal = 1.0 / scale + 2.0 + flat[None]
    rho = 2.0 / (diagonal + np.sqrt(diagonal * diagonal - 4.0))
    inverse = 1.0 / rho
    kappa = 1.0 / (scale * (inverse - rho))
    rho, inverse, kappa = (t.astype(np.float32) for t in (rho, inverse, kappa))
    rho_slab = (rho.astype(np.float64) ** block).astype(np.float32)
    rounds = 1
    while np.float32(float(rho.max()) ** (block * rounds)) > 0:
        rounds += 1

    depth_table = left_table(sine)
    x_table = right_table(sine)
    y_table = left_table(sine[:, order])
    back_table = left_table(sine[order, :])
    x_low_table = right_table(sine[:, :coarse])
    low_table = left_table(sine[:coarse, :])
    eigen = (DIFFUSION * (fine_w[:, None] + fine_w[None, :])).astype(np.float32)
    coarse_eigen = (0.25 * DIFFUSION * (coarse_w[:, None] + coarse_w[None, :])).astype(np.float32)
    fine_own = lax.dynamic_slice(jnp.asarray((DIFFUSION * fine_w[order]).astype(np.float32)), (group_index * block,), (block,))
    coarse_own = lax.dynamic_slice(
        jnp.asarray((0.25 * DIFFUSION * coarse_w).astype(np.float32)), (group_index * half,), (half,)
    )

    rows_spec = pl.BlockSpec((grid, ROWS, grid), lambda i: (0, i, 0))
    table_spec = whole_block(depth_table.shape)
    lengths = (block // 2, block - block // 2)
    begins = (0, block // 2)
    parts = len(lengths)
    end_begin = begins[1]

    def depth(chosen):
        span = slice(begins[chosen[0]], begins[chosen[-1]] + lengths[chosen[-1]])
        table = depth_table.reshape(groups, block, -1)[:, span].reshape(-1, depth_table.shape[1])
        return pl.pallas_call(
            depth_kernel,
            grid_spec=pltpu.PrefetchScalarGridSpec(
                num_scalar_prefetch=1,
                grid=(block // ROWS,),
                in_specs=[
                    whole_block(table.shape),
                    pl.BlockSpec((grid, ROWS, grid), lambda i, last: (0, i * last[0], 0)),
                    pl.BlockSpec((1, grid, ROWS, grid), lambda i, last: (0, 0, i * (1 - last[0]), 0)),
                ],
                out_specs=[
                    pl.BlockSpec((groups, lengths[part], ROWS, grid), lambda i, last: (0, 0, i, 0))
                    for part in chosen
                ],
            ),
            out_shape=[jax.ShapeDtypeStruct((groups, lengths[part], block, grid), F32) for part in chosen],
            compiler_params=pltpu.CompilerParams(vmem_limit_bytes=VMEM_BYTES),
            cost_estimate=pl.CostEstimate(flops=6 * unit * grid, bytes_accessed=8 * unit, transcendentals=0),
            name="depth",
        )(last, table, initial_modes, end_modes)

    outgoing = [*depth((0,)), *depth((1,))]
    outgoing[0] = turned(outgoing[0], "tm")

    pair = (2, grid, grid)
    pair_spec = whole_block(pair)
    whole = (groups, block, half)
    shapes = [
        (*whole, coarse),
        (groups, block - end_begin, half, grid + coarse),
        (4, block, grid, grid),
    ]
    arrays = None
    state = (np.ones(pair, np.float32), np.zeros(pair, np.float32), np.zeros(pair, np.float32))
    backs, states = {}, {}
    for part in reversed(range(parts)):
        given = outgoing[part]
        if part + 1 in backs:
            given, *_ = after(given, backs[part + 1], *states.get(part + 2, ()))
        backs[part] = exchange(given)
        modes = turned(backs[part], "tm") if part == parts - 1 else backs[part]
        steps = lengths[part] // planes
        bases = [begins[part] // planes] * 3
        if part >= 1:
            bases[1] = (begins[part] - end_begin) // planes
        else:
            shapes[1] = (groups, end_begin, half, grid + coarse)
        specs = [
            pl.BlockSpec(
                (4, planes, grid, grid) if n == 2 else (groups, planes, half, shapes[n][3]),
                lambda i, base=base, steps=steps: (0, base + steps - 1 - i, 0, 0),
            )
            for n, base in enumerate(bases)
        ]
        held = [n for n in range(3) if arrays is not None and not (part == 0 and n == 1)]
        outs = call(
            functools.partial(start_kernel, planes),
            "start",
            (steps,),
            [
                pl.BlockSpec((groups, planes, block, grid), lambda i, steps=steps: (0, steps - 1 - i, 0, 0)),
                whole_block(x_table.shape),
                table_spec,
                table_spec,
                pair_spec,
                pair_spec,
                pair_spec,
                pair_spec,
            ] + [pl.BlockSpec(memory_space=pl.ANY)] * len(held),
            specs + [pair_spec] * 3,
            [jax.ShapeDtypeStruct(shape, F32) for shape in shapes] + [jax.ShapeDtypeStruct(pair, F32)] * 3,
            scratch=[pltpu.VMEM((planes, grid, grid), F32)],
            flops=24 * unit * grid * lengths[part] // block,
            moved=24 * unit * lengths[part] // block,
            aliases={8 + place: n for place, n in enumerate(held)},
        )(modes, x_table, y_table, back_table, rho, *state, *(arrays[n] for n in held))
        if part >= 1:
            rest_last = outs[1]
        else:
            rest_first = outs[1]
        arrays, state = outs[:3], outs[3:]
        states[part] = state
    corner, _, v = arrays
    _, to_right, to_left = state
    rest_last, backs[0] = after(rest_last, backs[0])
    rest_last_back = exchange(rest_last)
    if rounds <= 2 and groups % 2 == 0:
        odd = group_index % 2 == 1
        swap = [(i, i ^ 1) for i in range(groups)]
        partner_right = lax.ppermute(to_right, "gx", swap)
        partner_left = lax.ppermute(to_left, "gx", swap)
        rightward = jnp.where(odd, to_right + rho_slab * partner_right, partner_right + rho_slab * to_right)
        leftward = jnp.where(odd, partner_left + rho_slab * to_left, to_left + rho_slab * partner_left)
        rightward, leftward = after(rightward, leftward)
        before, behind = after(shifted(rightward, "gx", 2), shifted(leftward, "gx", -2))
        before = jnp.where(group_index < 2, -rho * leftward, before)
        behind = jnp.where(group_index >= groups - 2, -rho * rightward, behind)
        from_left = jnp.where(odd, partner_right + rho_slab * before, before)
        from_right = jnp.where(odd, behind, partner_left + rho_slab * behind)
    else:
        at_start, at_end = group_index == 0, group_index == groups - 1
        from_left = jnp.zeros(pair, F32)
        from_right = jnp.zeros(pair, F32)
        for _ in range(rounds):
            rightward = to_right + rho_slab * from_left
            leftward = to_left + rho_slab * from_right
            from_left = jnp.where(at_start, -rho * leftward, shifted(rightward, "gx", 1))
            from_right = jnp.where(at_end, -rho * rightward, shifted(leftward, "gx", -1))

    corner, rest_last_back, from_left, from_right = after(corner, rest_last_back, from_left, from_right)
    corner_back = exchange(corner.reshape(grid, half, coarse))
    cubic = call(
        functools.partial(node_kernel, planes, block),
        "nodes",
        (block // planes,),
        [pl.BlockSpec((4, planes, grid, grid), lambda i: (0, i, 0, 0))]
        + [pair_spec] * 5
        + [
            whole_block(x_table.shape),
            table_spec,
            whole_block(x_low_table.shape),
            whole_block(low_table.shape),
        ],
        pl.BlockSpec((groups, planes, half, coarse), lambda i: (0, i, 0, 0)),
        jax.ShapeDtypeStruct((groups, block, half, coarse), F32),
        scratch=[pltpu.VMEM(pair, F32), pltpu.VMEM(pair, F32), pltpu.VMEM((2, planes, grid, grid), F32)],
        flops=28 * unit * grid,
        moved=17 * unit,
    )(v, from_left, from_right, rho, inverse, kappa, x_table, y_table, x_low_table, low_table)
    cubic, corner_back = after(cubic, corner_back)
    cubic_back = exchange(cubic.reshape(grid, half, coarse))
    rest_first, cubic_back = after(rest_first, cubic_back)
    rest_backs = [exchange(rest_first), rest_last_back]
    start_low = jnp.where(
        is_first, initial_modes[:coarse, :half, :coarse], shifted(end_modes[0, :coarse, :half, :coarse], "tm", 1)
    )

    low_spec = pl.BlockSpec((coarse, ROWS, coarse), lambda i: (0, i, 0))
    coarse_eigen_spec = whole_block(coarse_eigen.shape)
    quarter_spec = pl.BlockSpec((grid, ROWS, coarse), lambda i: (0, i, 0))
    corner_shape = jax.ShapeDtypeStruct((coarse, half, coarse), F32)
    result_shape = jax.ShapeDtypeStruct((grid, block, grid), F32)
    corner_end, gathered = call(
        functools.partial(low_kernel, factor),
        "low",
        (half // ROWS,),
        [SMEM, SMEM, table_spec, whole_block((grid, coarse)), coarse_eigen_spec, quarter_spec, low_spec],
        [low_spec, low_spec],
        [corner_shape, corner_shape],
        flops=2 * unit * grid,
        moved=3 * unit,
    )(fine_own, coarse_own, depth_table, eigen[:, :coarse], coarse_eigen, corner_back, start_low)
    offset = call(
        functools.partial(offset_kernel, factor),
        "offset",
        (half // ROWS,),
        [SMEM, SMEM, whole_block(low_table.shape), coarse_eigen_spec, low_spec, low_spec, quarter_spec],
        low_spec,
        corner_shape,
        flops=unit * grid,
        moved=2 * unit,
    )(first, coarse_own, low_table, coarse_eigen, gathered, start_low, cubic_back)

    decay = 1.0 / (1.0 + coarse_eigen[:, None, :] + coarse_own[None, :, None])
    coarse_end = offset
    for turn in range(1, slices):
        incoming = lax.ppermute(coarse_end, "tm", [(turn - 1, turn)])
        coarse_end = jnp.where(slice_index == turn, decay * incoming + offset, coarse_end)
    turns = half // ROWS
    upper = [
        pl.BlockSpec((groups, part.shape[1], ROWS, coarse), lambda i, n=n: (0, 0, jnp.minimum(i, turns - 1), n))
        for n in range(2)
        for part in rest_backs
    ]
    side = [
        pl.BlockSpec((groups, part.shape[1], ROWS, coarse), lambda i: (0, 0, jnp.maximum(i - turns, 0), 2))
        for part in rest_backs
    ]
    corner_spec = pl.BlockSpec((coarse, ROWS, coarse), lambda i: (0, jnp.maximum(i - turns, 0), 0))
    result = call(
        functools.partial(finish_kernel, factor),
        "finish",
        (2 * turns,),
        [SMEM, table_spec, whole_block(eigen.shape), corner_spec, corner_spec] + upper + side,
        pl.BlockSpec((grid, ROWS, grid), lambda i: (0, (i + turns) % (2 * turns), 0)),
        result_shape,
        flops=5 * unit * grid,
        moved=9 * unit,
    )(fine_own, depth_table, eigen, corner_end, coarse_end, *(rest_backs * 3))
    return (result[None], coarse_end[None])


def solution(mesh):
    return jax.shard_map(
        per_device,
        mesh=mesh,
        in_specs=(P("tm", None, "gx", None), P(None, "gx", None)),
        out_specs=(P("tm", None, "gx", None), P("tm", None, "gx", None)),
        check_vma=False,
    )
```

```python
import functools
import math

import jax
import jax.numpy as jnp
import ml_dtypes
import numpy as np
from jax import lax
from jax.experimental import pallas as pl
from jax.experimental.pallas import tpu as pltpu
from jax.sharding import PartitionSpec as P

DIFFUSION = 0.25
BF16 = jnp.bfloat16
F32 = jnp.float32
ROWS = 8
VMEM_BYTES = 56 * 1024 * 1024


def sine_matrix(length):
    index = np.arange(1, length + 1)
    phase = np.outer(index, index) % (2 * (length + 1))
    return np.sin(phase * (math.pi / (length + 1))) * math.sqrt(2.0 / (length + 1))


def omega(count):
    return 2.0 - 2.0 * np.cos((np.arange(count) + 1.0) * (math.pi / (count + 1)))


def fine_order(grid, groups):
    block, coarse = grid // groups, grid // 2
    half = block // 2
    position = np.arange(grid)
    within, group = position % block, position // block
    return np.where(within < half, group * half + within, coarse + group * half + within - half)


def halves(table):
    high = table.astype(ml_dtypes.bfloat16)
    low = (table - high.astype(np.float64)).astype(ml_dtypes.bfloat16)
    return high, low


def left_table(table):
    high, low = halves(table)
    return np.concatenate([high, high, low], axis=1)


def right_table(table):
    high, low = halves(table)
    return np.concatenate([high, high, low], axis=0)


def split3(value, axis):
    high = value.astype(BF16)
    low = (value - high.astype(F32)).astype(BF16)
    return jnp.concatenate([high, low, high], axis=axis)


def left(table, value):
    return jnp.dot(table, split3(value, 0), preferred_element_type=F32)


def right(value, table):
    return jnp.dot(split3(value, 1), table, preferred_element_type=F32)


def cube(value):
    return value * value * value


def whole_block(shape):
    return pl.BlockSpec(shape, lambda *_: (0,) * len(shape))


SMEM = pl.BlockSpec(memory_space=pltpu.SMEM)


def call(kernel, name, grid, in_specs, out_specs, out_shape, scratch=(), flops=0, moved=0, aliases=None):
    return pl.pallas_call(
        kernel,
        grid=grid,
        in_specs=in_specs,
        out_specs=out_specs,
        out_shape=out_shape,
        scratch_shapes=list(scratch),
        input_output_aliases=aliases or {},
        compiler_params=pltpu.CompilerParams(vmem_limit_bytes=VMEM_BYTES),
        cost_estimate=pl.CostEstimate(flops=flops, bytes_accessed=moved, transcendentals=0),
        name=name,
    )


def depth_kernel(last_ref, table_ref, initial_ref, end_ref, *out_refs):
    value = jnp.swapaxes(jnp.where(last_ref[0] == 1, initial_ref[...], end_ref[0]), 0, 1)
    rows = jnp.stack([left(table_ref[...], value[row]) for row in range(ROWS)])
    groups, _, _, wide = out_refs[0].shape
    rows = jnp.swapaxes(rows, 0, 1).reshape(groups, -1, ROWS, wide)
    begin = 0
    for out_ref in out_refs:
        planes = out_ref.shape[1]
        out_ref[...] = rows[:, begin:begin + planes]
        begin += planes


def start_kernel(planes, modes_ref, sx_ref, sy_ref, syt_ref, rho_ref, power_ref, right_ref, left_ref, *refs):
    corner_ref, rest_ref, v_ref, power, to_right_ref, to_left_ref, cubic = refs[-7:]

    @pl.when(pl.program_id(0) == 0)
    def _():
        power[...] = power_ref[...]
        to_right_ref[...] = right_ref[...]
        to_left_ref[...] = left_ref[...]

    groups, _, block, wide = modes_ref.shape
    grid = groups * block
    half = block // 2
    modes = [modes_ref[:, j].reshape(grid, wide) for j in range(planes)]
    along_x = right(jnp.concatenate(modes, axis=0), sx_ref[...])
    terms = [cube(left(sy_ref[...], along_x[j * grid:(j + 1) * grid])) for j in range(planes)]
    along_x = right(jnp.concatenate(terms, axis=0), sx_ref[...])
    for j in range(planes):
        cubic[j] = left(syt_ref[...], along_x[j * grid:(j + 1) * grid])
    for strip in range(2 * groups):
        group, upper = strip // 2, strip % 2
        rows = slice(strip * half, (strip + 1) * half)
        within = slice(upper * half, (upper + 1) * half)
        rho = [rho_ref[node, rows] for node in range(2)]
        carried = [to_left_ref[node, rows] for node in range(2)]
        weight = [power[node, rows] for node in range(2)]
        total = [to_right_ref[node, rows] for node in range(2)]
        for j in reversed(range(planes)):
            mode = modes_ref[group, j, within]
            source = 2.0 * mode - cubic[j, rows]
            if upper:
                rest_ref[group, j, :, :wide] = source
            else:
                corner_ref[group, j] = source[:, :wide // 2]
                rest_ref[group, j, :, wide:] = source[:, wide // 2:]
            for node, value in enumerate((source, 0.5 * (mode + source))):
                carried[node] = value + rho[node] * carried[node]
                v_ref[node, j, rows] = carried[node]
                v_ref[2 + node, j, rows] = value
                total[node] += weight[node] * value
                weight[node] = weight[node] * rho[node]
        for node in range(2):
            to_left_ref[node, rows] = carried[node]
            power[node, rows] = weight[node]
            to_right_ref[node, rows] = total[node]


def node_kernel(planes, slab, v_ref, from_left_ref, from_right_ref, rho_ref, inverse_ref, kappa_ref,
                sx_ref, sy_ref, sxl_ref, syl_ref, out_ref, left_sum, right_sum, nodes):
    step = pl.program_id(0)
    plane = step * planes

    @pl.when(step == 0)
    def _():
        left_sum[...] = from_left_ref[...]

    @pl.when(plane % ROWS == 0)
    def _():
        rho = rho_ref[...]
        twice = rho * rho
        four = twice * twice
        eight = four * four
        right_sum[...] = lax.fori_loop(
            0, slab // ROWS - plane // ROWS, lambda _, total: total * eight, from_right_ref[...]
        )

    groups, _, half, low = out_ref.shape
    grid = v_ref.shape[2]
    wide = v_ref.shape[3]
    for strip in range(2 * groups):
        rows = slice(strip * half, (strip + 1) * half)
        rho = [rho_ref[node, rows] for node in range(2)]
        inverse = [inverse_ref[node, rows] for node in range(2)]
        kappa = [kappa_ref[node, rows] for node in range(2)]
        before = [left_sum[node, rows] for node in range(2)]
        after = [right_sum[node, rows] for node in range(2)]
        for j in range(planes):
            for node in range(2):
                behind = rho[node] * before[node]
                before[node] = v_ref[2 + node, j, rows] + behind
                nodes[node, j, rows] = kappa[node] * (behind + v_ref[node, j, rows] + after[node])
                after[node] = after[node] * inverse[node]
        for node in range(2):
            left_sum[node, rows] = before[node]
            right_sum[node, rows] = after[node]
    along_x = right(nodes[...].reshape(2 * planes * grid, wide), sx_ref[...])
    fields = [left(sy_ref[...], along_x[j * grid:(j + 1) * grid]) for j in range(2 * planes)]
    terms = [cube(fields[j]) + 4.0 * cube(fields[planes + j]) for j in range(planes)]
    along_x = right(jnp.concatenate(terms, axis=0), sxl_ref[...])
    for j in range(planes):
        term = left(syl_ref[...], along_x[j * grid:(j + 1) * grid])
        out_ref[:, j] = term.reshape(groups, half, low)


def joined(refs):
    parts = jnp.concatenate([ref[...] for ref in refs], axis=1)
    return parts.reshape(parts.shape[0] * parts.shape[1], *parts.shape[2:])


def low_kernel(factor, fine_ref, coarse_ref, table_ref, eigen_ref, coarse_eigen_ref, corner_ref, start_ref,
               out_ref, gathered_ref):
    base = pl.program_id(0) * ROWS
    coarse = start_ref.shape[0]
    sources = jnp.swapaxes(corner_ref[...], 0, 1)
    starts = jnp.swapaxes(start_ref[...], 0, 1)
    ends, gathered = [], []
    for row in range(ROWS):
        source = left(table_ref[...], sources[row])
        eigen = eigen_ref[...] + fine_ref[base + row]
        node_end = source / (1.0 + eigen)
        ends.append(node_end[coarse:])
        source, node_end, eigen = source[:coarse], node_end[:coarse], eigen[:coarse]
        start = starts[row]
        node_mid = 0.5 * (start + source) / (1.0 + 0.5 * eigen)
        rate = source - (1.0 + eigen) * start + (1.0 - eigen) * (4.0 * node_mid + node_end)
        coarse_eigen = coarse_eigen_ref[...] + coarse_ref[base + row]
        gathered.append(factor * (rate / 6.0 + coarse_eigen * node_end))
    out_ref[...] = jnp.swapaxes(jnp.stack(ends), 0, 1)
    gathered_ref[...] = jnp.swapaxes(jnp.stack(gathered), 0, 1)


def offset_kernel(factor, first_ref, coarse_ref, table_ref, coarse_eigen_ref, gathered_ref, start_ref, cubic_ref,
                  out_ref):
    base = pl.program_id(0) * ROWS
    first = first_ref[0] == 1
    cubics = jnp.swapaxes(cubic_ref[...], 0, 1)
    given = jnp.swapaxes(gathered_ref[...] + jnp.where(first, factor * start_ref[...], 0.0), 0, 1)
    rows = []
    for row in range(ROWS):
        total = given[row] - (factor / 6.0) * left(table_ref[...], cubics[row])
        rows.append(total / (1.0 + coarse_eigen_ref[...] + coarse_ref[base + row]))
    out_ref[...] = jnp.swapaxes(jnp.stack(rows), 0, 1)


def finish_kernel(factor, fine_ref, table_ref, eigen_ref, corner_ref, end_ref, *refs):
    out_ref = refs[-1]
    coarse = end_ref.shape[0]
    steps = pl.num_programs(0) // 2
    step = pl.program_id(0)
    base = (step + steps) % (2 * steps) * ROWS
    fields = [joined(refs[n:n + 2]) for n in range(0, 6, 2)]

    def solved(source, eigen):
        source = jnp.swapaxes(source, 0, 1)
        rows = [left(table_ref[...], source[row]) / (1.0 + eigen + fine_ref[base + row]) for row in range(ROWS)]
        return jnp.swapaxes(jnp.stack(rows), 0, 1)

    @pl.when(step < steps)
    def _():
        out_ref[...] = solved(jnp.concatenate(fields[:2], axis=2), eigen_ref[...])

    @pl.when(step >= steps)
    def _():
        out_ref[:coarse, :, :coarse] = end_ref[...] / factor
        out_ref[coarse:, :, :coarse] = corner_ref[...]
        out_ref[:, :, coarse:] = solved(fields[2], eigen_ref[:, coarse:])


def shifted(value, axis, by):
    length = lax.axis_size(axis)
    pairs = [(i, i + by) for i in range(length) if 0 <= i + by < length]
    return lax.ppermute(value, axis, pairs)


def turned(value, axis):
    length = lax.axis_size(axis)
    return lax.ppermute(value, axis, [(i, (i + 1) % length) for i in range(length)])


def exchange(value):
    return lax.all_to_all(value, "gx", split_axis=0, concat_axis=0, tiled=True)


def after(value, *earlier):
    return lax.optimization_barrier((value, *earlier))


def per_device(end_modes, initial_modes):
    grid = initial_modes.shape[0]
    coarse = grid // 2
    groups = lax.axis_size("gx")
    block = grid // groups
    half = block // 2
    planes = 2
    slice_index = lax.axis_index("tm")
    group_index = lax.axis_index("gx")
    is_first = slice_index == 0
    slices = lax.axis_size("tm")
    first = is_first.astype(jnp.int32)[None]
    last = (slice_index == slices - 1).astype(jnp.int32)[None]
    order = fine_order(grid, groups)
    sine = sine_matrix(grid)
    fine_w, coarse_w = omega(grid), omega(coarse)
    factor = ((coarse + 1) / (grid + 1)) ** 1.5
    unit = grid * block * grid

    flat = fine_w[order][:, None] + fine_w[None, :]
    scale = np.array([1.0, 0.5])[:, None, None] * DIFFUSION
    diagonal = 1.0 / scale + 2.0 + flat[None]
    rho = 2.0 / (diagonal + np.sqrt(diagonal * diagonal - 4.0))
    inverse = 1.0 / rho
    kappa = 1.0 / (scale * (inverse - rho))
    rho, inverse, kappa = (t.astype(np.float32) for t in (rho, inverse, kappa))
    rho_slab = (rho.astype(np.float64) ** block).astype(np.float32)
    rounds = 1
    while np.float32(float(rho.max()) ** (block * rounds)) > 0:
        rounds += 1

    depth_table = left_table(sine)
    x_table = right_table(sine)
    y_table = left_table(sine[:, order])
    back_table = left_table(sine[order, :])
    x_low_table = right_table(sine[:, :coarse])
    low_table = left_table(sine[:coarse, :])
    eigen = (DIFFUSION * (fine_w[:, None] + fine_w[None, :])).astype(np.float32)
    coarse_eigen = (0.25 * DIFFUSION * (coarse_w[:, None] + coarse_w[None, :])).astype(np.float32)
    fine_own = lax.dynamic_slice(jnp.asarray((DIFFUSION * fine_w[order]).astype(np.float32)), (group_index * block,), (block,))
    coarse_own = lax.dynamic_slice(
        jnp.asarray((0.25 * DIFFUSION * coarse_w).astype(np.float32)), (group_index * half,), (half,)
    )

    rows_spec = pl.BlockSpec((grid, ROWS, grid), lambda i: (0, i, 0))
    table_spec = whole_block(depth_table.shape)
    shorter = 7 * block // 16 // planes * planes
    lengths = (shorter, block - shorter)
    begins = (0, shorter)
    parts = len(lengths)
    end_begin = begins[1]

    def depth(chosen):
        span = slice(begins[chosen[0]], begins[chosen[-1]] + lengths[chosen[-1]])
        table = depth_table.reshape(groups, block, -1)[:, span].reshape(-1, depth_table.shape[1])
        return pl.pallas_call(
            depth_kernel,
            grid_spec=pltpu.PrefetchScalarGridSpec(
                num_scalar_prefetch=1,
                grid=(block // ROWS,),
                in_specs=[
                    whole_block(table.shape),
                    pl.BlockSpec((grid, ROWS, grid), lambda i, last: (0, i * last[0], 0)),
                    pl.BlockSpec((1, grid, ROWS, grid), lambda i, last: (0, 0, i * (1 - last[0]), 0)),
                ],
                out_specs=[
                    pl.BlockSpec((groups, lengths[part], ROWS, grid), lambda i, last: (0, 0, i, 0))
                    for part in chosen
                ],
            ),
            out_shape=[jax.ShapeDtypeStruct((groups, lengths[part], block, grid), F32) for part in chosen],
            compiler_params=pltpu.CompilerParams(vmem_limit_bytes=VMEM_BYTES),
            cost_estimate=pl.CostEstimate(flops=6 * unit * grid, bytes_accessed=8 * unit, transcendentals=0),
            name="depth",
        )(last, table, initial_modes, end_modes)

    outgoing = [*depth((0,)), *depth((1,))]
    outgoing[0] = turned(outgoing[0], "tm")

    pair = (2, grid, grid)
    pair_spec = whole_block(pair)
    whole = (groups, block, half)
    shapes = [
        (*whole, coarse),
        (groups, block - end_begin, half, grid + coarse),
        (4, block, grid, grid),
    ]
    arrays = None
    state = (np.ones(pair, np.float32), np.zeros(pair, np.float32), np.zeros(pair, np.float32))
    backs, states = {}, {}
    for part in reversed(range(parts)):
        given = outgoing[part]
        if part + 1 in backs:
            given, *_ = after(given, backs[part + 1], *states.get(part + 2, ()))
        backs[part] = exchange(given)
        modes = turned(backs[part], "tm") if part == parts - 1 else backs[part]
        steps = lengths[part] // planes
        bases = [begins[part] // planes] * 3
        if part >= 1:
            bases[1] = (begins[part] - end_begin) // planes
        else:
            shapes[1] = (groups, end_begin, half, grid + coarse)
        specs = [
            pl.BlockSpec(
                (4, planes, grid, grid) if n == 2 else (groups, planes, half, shapes[n][3]),
                lambda i, base=base, steps=steps: (0, base + steps - 1 - i, 0, 0),
            )
            for n, base in enumerate(bases)
        ]
        held = [n for n in range(3) if arrays is not None and not (part == 0 and n == 1)]
        outs = call(
            functools.partial(start_kernel, planes),
            "start",
            (steps,),
            [
                pl.BlockSpec((groups, planes, block, grid), lambda i, steps=steps: (0, steps - 1 - i, 0, 0)),
                whole_block(x_table.shape),
                table_spec,
                table_spec,
                pair_spec,
                pair_spec,
                pair_spec,
                pair_spec,
            ] + [pl.BlockSpec(memory_space=pl.ANY)] * len(held),
            specs + [pair_spec] * 3,
            [jax.ShapeDtypeStruct(shape, F32) for shape in shapes] + [jax.ShapeDtypeStruct(pair, F32)] * 3,
            scratch=[pltpu.VMEM((planes, grid, grid), F32)],
            flops=24 * unit * grid * lengths[part] // block,
            moved=24 * unit * lengths[part] // block,
            aliases={8 + place: n for place, n in enumerate(held)},
        )(modes, x_table, y_table, back_table, rho, *state, *(arrays[n] for n in held))
        if part >= 1:
            rest_last = outs[1]
        else:
            rest_first = outs[1]
        arrays, state = outs[:3], outs[3:]
        states[part] = state
    corner, _, v = arrays
    _, to_right, to_left = state
    rest_last, backs[0] = after(rest_last, backs[0])
    rest_last_back = exchange(rest_last)
    if rounds <= 2 and groups % 2 == 0:
        odd = group_index % 2 == 1
        swap = [(i, i ^ 1) for i in range(groups)]
        partner_right = lax.ppermute(to_right, "gx", swap)
        partner_left = lax.ppermute(to_left, "gx", swap)
        rightward = jnp.where(odd, to_right + rho_slab * partner_right, partner_right + rho_slab * to_right)
        leftward = jnp.where(odd, partner_left + rho_slab * to_left, to_left + rho_slab * partner_left)
        rightward, leftward = after(rightward, leftward)
        before, behind = after(shifted(rightward, "gx", 2), shifted(leftward, "gx", -2))
        before = jnp.where(group_index < 2, -rho * leftward, before)
        behind = jnp.where(group_index >= groups - 2, -rho * rightward, behind)
        from_left = jnp.where(odd, partner_right + rho_slab * before, before)
        from_right = jnp.where(odd, behind, partner_left + rho_slab * behind)
    else:
        at_start, at_end = group_index == 0, group_index == groups - 1
        from_left = jnp.zeros(pair, F32)
        from_right = jnp.zeros(pair, F32)
        for _ in range(rounds):
            rightward = to_right + rho_slab * from_left
            leftward = to_left + rho_slab * from_right
            from_left = jnp.where(at_start, -rho * leftward, shifted(rightward, "gx", 1))
            from_right = jnp.where(at_end, -rho * rightward, shifted(leftward, "gx", -1))

    corner, rest_last_back, from_left, from_right = after(corner, rest_last_back, from_left, from_right)
    corner_back = exchange(corner.reshape(grid, half, coarse))
    cubic = call(
        functools.partial(node_kernel, planes, block),
        "nodes",
        (block // planes,),
        [pl.BlockSpec((4, planes, grid, grid), lambda i: (0, i, 0, 0))]
        + [pair_spec] * 5
        + [
            whole_block(x_table.shape),
            table_spec,
            whole_block(x_low_table.shape),
            whole_block(low_table.shape),
        ],
        pl.BlockSpec((groups, planes, half, coarse), lambda i: (0, i, 0, 0)),
        jax.ShapeDtypeStruct((groups, block, half, coarse), F32),
        scratch=[pltpu.VMEM(pair, F32), pltpu.VMEM(pair, F32), pltpu.VMEM((2, planes, grid, grid), F32)],
        flops=28 * unit * grid,
        moved=17 * unit,
    )(v, from_left, from_right, rho, inverse, kappa, x_table, y_table, x_low_table, low_table)
    cubic, corner_back = after(cubic, corner_back)
    cubic_back = exchange(cubic.reshape(grid, half, coarse))
    rest_first, cubic_back = after(rest_first, cubic_back)
    rest_backs = [exchange(rest_first), rest_last_back]
    start_low = jnp.where(
        is_first, initial_modes[:coarse, :half, :coarse], shifted(end_modes[0, :coarse, :half, :coarse], "tm", 1)
    )

    low_spec = pl.BlockSpec((coarse, ROWS, coarse), lambda i: (0, i, 0))
    coarse_eigen_spec = whole_block(coarse_eigen.shape)
    quarter_spec = pl.BlockSpec((grid, ROWS, coarse), lambda i: (0, i, 0))
    corner_shape = jax.ShapeDtypeStruct((coarse, half, coarse), F32)
    result_shape = jax.ShapeDtypeStruct((grid, block, grid), F32)
    corner_end, gathered = call(
        functools.partial(low_kernel, factor),
        "low",
        (half // ROWS,),
        [SMEM, SMEM, table_spec, whole_block((grid, coarse)), coarse_eigen_spec, quarter_spec, low_spec],
        [low_spec, low_spec],
        [corner_shape, corner_shape],
        flops=2 * unit * grid,
        moved=3 * unit,
    )(fine_own, coarse_own, depth_table, eigen[:, :coarse], coarse_eigen, corner_back, start_low)
    offset = call(
        functools.partial(offset_kernel, factor),
        "offset",
        (half // ROWS,),
        [SMEM, SMEM, whole_block(low_table.shape), coarse_eigen_spec, low_spec, low_spec, quarter_spec],
        low_spec,
        corner_shape,
        flops=unit * grid,
        moved=2 * unit,
    )(first, coarse_own, low_table, coarse_eigen, gathered, start_low, cubic_back)

    decay = 1.0 / (1.0 + coarse_eigen[:, None, :] + coarse_own[None, :, None])
    coarse_end = offset
    for turn in range(1, slices):
        incoming = lax.ppermute(coarse_end, "tm", [(turn - 1, turn)])
        coarse_end = jnp.where(slice_index == turn, decay * incoming + offset, coarse_end)
    turns = half // ROWS
    upper = [
        pl.BlockSpec((groups, part.shape[1], ROWS, coarse), lambda i, n=n: (0, 0, jnp.minimum(i, turns - 1), n))
        for n in range(2)
        for part in rest_backs
    ]
    side = [
        pl.BlockSpec((groups, part.shape[1], ROWS, coarse), lambda i: (0, 0, jnp.maximum(i - turns, 0), 2))
        for part in rest_backs
    ]
    corner_spec = pl.BlockSpec((coarse, ROWS, coarse), lambda i: (0, jnp.maximum(i - turns, 0), 0))
    result = call(
        functools.partial(finish_kernel, factor),
        "finish",
        (2 * turns,),
        [SMEM, table_spec, whole_block(eigen.shape), corner_spec, corner_spec] + upper + side,
        pl.BlockSpec((grid, ROWS, grid), lambda i: (0, (i + turns) % (2 * turns), 0)),
        result_shape,
        flops=5 * unit * grid,
        moved=9 * unit,
    )(fine_own, depth_table, eigen, corner_end, coarse_end, *(rest_backs * 3))
    return (result[None], coarse_end[None])


def solution(mesh):
    return jax.shard_map(
        per_device,
        mesh=mesh,
        in_specs=(P("tm", None, "gx", None), P(None, "gx", None)),
        out_specs=(P("tm", None, "gx", None), P("tm", None, "gx", None)),
        check_vma=False,
    )
```

```python
import functools
import math

import jax
import jax.numpy as jnp
import ml_dtypes
import numpy as np
from jax import lax
from jax.experimental import pallas as pl
from jax.experimental.pallas import tpu as pltpu
from jax.sharding import PartitionSpec as P

DIFFUSION = 0.25
BF16 = jnp.bfloat16
F32 = jnp.float32
ROWS = 8
VMEM_BYTES = 56 * 1024 * 1024


def sine_matrix(length):
    index = np.arange(1, length + 1)
    phase = np.outer(index, index) % (2 * (length + 1))
    return np.sin(phase * (math.pi / (length + 1))) * math.sqrt(2.0 / (length + 1))


def omega(count):
    return 2.0 - 2.0 * np.cos((np.arange(count) + 1.0) * (math.pi / (count + 1)))


def fine_order(grid, groups):
    block, coarse = grid // groups, grid // 2
    half = block // 2
    position = np.arange(grid)
    within, group = position % block, position // block
    return np.where(within < half, group * half + within, coarse + group * half + within - half)


def halves(table):
    high = table.astype(ml_dtypes.bfloat16)
    low = (table - high.astype(np.float64)).astype(ml_dtypes.bfloat16)
    return high, low


def left_table(table):
    high, low = halves(table)
    return np.concatenate([high, high, low], axis=1)


def right_table(table):
    high, low = halves(table)
    return np.concatenate([high, high, low], axis=0)


def split3(value, axis):
    high = value.astype(BF16)
    low = (value - high.astype(F32)).astype(BF16)
    return jnp.concatenate([high, low, high], axis=axis)


def left(table, value):
    return jnp.dot(table, split3(value, 0), preferred_element_type=F32)


def right(value, table):
    return jnp.dot(split3(value, 1), table, preferred_element_type=F32)


def cube(value):
    return value * value * value


def whole_block(shape):
    return pl.BlockSpec(shape, lambda *_: (0,) * len(shape))


SMEM = pl.BlockSpec(memory_space=pltpu.SMEM)


def call(kernel, name, grid, in_specs, out_specs, out_shape, scratch=(), flops=0, moved=0, aliases=None):
    return pl.pallas_call(
        kernel,
        grid=grid,
        in_specs=in_specs,
        out_specs=out_specs,
        out_shape=out_shape,
        scratch_shapes=list(scratch),
        input_output_aliases=aliases or {},
        compiler_params=pltpu.CompilerParams(vmem_limit_bytes=VMEM_BYTES),
        cost_estimate=pl.CostEstimate(flops=flops, bytes_accessed=moved, transcendentals=0),
        name=name,
    )


def depth_kernel(last_ref, table_ref, initial_ref, end_ref, *out_refs):
    value = jnp.swapaxes(jnp.where(last_ref[0] == 1, initial_ref[...], end_ref[0]), 0, 1)
    rows = jnp.stack([left(table_ref[...], value[row]) for row in range(ROWS)])
    groups, _, _, wide = out_refs[0].shape
    rows = jnp.swapaxes(rows, 0, 1).reshape(groups, -1, ROWS, wide)
    begin = 0
    for out_ref in out_refs:
        planes = out_ref.shape[1]
        out_ref[...] = rows[:, begin:begin + planes]
        begin += planes


def start_kernel(planes, modes_ref, sx_ref, sy_ref, syt_ref, rho_ref, power_ref, right_ref, left_ref, *refs):
    corner_ref, rest_ref, v_ref, power, to_right_ref, to_left_ref, cubic = refs[-7:]

    @pl.when(pl.program_id(0) == 0)
    def _():
        power[...] = power_ref[...]
        to_right_ref[...] = right_ref[...]
        to_left_ref[...] = left_ref[...]

    groups, _, block, wide = modes_ref.shape
    grid = groups * block
    half = block // 2
    modes = [modes_ref[:, j].reshape(grid, wide) for j in range(planes)]
    along_x = right(jnp.concatenate(modes, axis=0), sx_ref[...])
    terms = [cube(left(sy_ref[...], along_x[j * grid:(j + 1) * grid])) for j in range(planes)]
    along_x = right(jnp.concatenate(terms, axis=0), sx_ref[...])
    for j in range(planes):
        cubic[j] = left(syt_ref[...], along_x[j * grid:(j + 1) * grid])
    for strip in range(2 * groups):
        group, upper = strip // 2, strip % 2
        rows = slice(strip * half, (strip + 1) * half)
        within = slice(upper * half, (upper + 1) * half)
        rho = [rho_ref[node, rows] for node in range(2)]
        carried = [to_left_ref[node, rows] for node in range(2)]
        weight = [power[node, rows] for node in range(2)]
        total = [to_right_ref[node, rows] for node in range(2)]
        for j in reversed(range(planes)):
            mode = modes_ref[group, j, within]
            source = 2.0 * mode - cubic[j, rows]
            if upper:
                rest_ref[group, j, :, :wide] = source
            else:
                corner_ref[group, j] = source[:, :wide // 2]
                rest_ref[group, j, :, wide:] = source[:, wide // 2:]
            for node, value in enumerate((source, 0.5 * (mode + source))):
                carried[node] = value + rho[node] * carried[node]
                v_ref[node, j, rows] = carried[node]
                v_ref[2 + node, j, rows] = value
                total[node] += weight[node] * value
                weight[node] = weight[node] * rho[node]
        for node in range(2):
            to_left_ref[node, rows] = carried[node]
            power[node, rows] = weight[node]
            to_right_ref[node, rows] = total[node]


def node_kernel(planes, slab, v_ref, from_left_ref, from_right_ref, rho_ref, inverse_ref, kappa_ref,
                sx_ref, sy_ref, sxl_ref, syl_ref, out_ref, left_sum, right_sum, nodes):
    step = pl.program_id(0)
    plane = step * planes

    @pl.when(step == 0)
    def _():
        left_sum[...] = from_left_ref[...]

    @pl.when(plane % ROWS == 0)
    def _():
        rho = rho_ref[...]
        twice = rho * rho
        four = twice * twice
        eight = four * four
        right_sum[...] = lax.fori_loop(
            0, slab // ROWS - plane // ROWS, lambda _, total: total * eight, from_right_ref[...]
        )

    groups, _, half, low = out_ref.shape
    grid = v_ref.shape[2]
    wide = v_ref.shape[3]
    for strip in range(2 * groups):
        rows = slice(strip * half, (strip + 1) * half)
        rho = [rho_ref[node, rows] for node in range(2)]
        inverse = [inverse_ref[node, rows] for node in range(2)]
        kappa = [kappa_ref[node, rows] for node in range(2)]
        before = [left_sum[node, rows] for node in range(2)]
        after = [right_sum[node, rows] for node in range(2)]
        for j in range(planes):
            for node in range(2):
                behind = rho[node] * before[node]
                before[node] = v_ref[2 + node, j, rows] + behind
                nodes[node, j, rows] = kappa[node] * (behind + v_ref[node, j, rows] + after[node])
                after[node] = after[node] * inverse[node]
        for node in range(2):
            left_sum[node, rows] = before[node]
            right_sum[node, rows] = after[node]
    along_x = right(nodes[...].reshape(2 * planes * grid, wide), sx_ref[...])
    fields = [left(sy_ref[...], along_x[j * grid:(j + 1) * grid]) for j in range(2 * planes)]
    terms = [cube(fields[j]) + 4.0 * cube(fields[planes + j]) for j in range(planes)]
    along_x = right(jnp.concatenate(terms, axis=0), sxl_ref[...])
    for j in range(planes):
        term = left(syl_ref[...], along_x[j * grid:(j + 1) * grid])
        out_ref[:, j] = term.reshape(groups, half, low)


def joined(refs):
    parts = jnp.concatenate([ref[...] for ref in refs], axis=1)
    return parts.reshape(parts.shape[0] * parts.shape[1], *parts.shape[2:])


def low_kernel(factor, fine_ref, coarse_ref, table_ref, eigen_ref, coarse_eigen_ref, corner_ref, start_ref,
               out_ref, gathered_ref):
    base = pl.program_id(0) * ROWS
    coarse = start_ref.shape[0]
    sources = jnp.swapaxes(corner_ref[...], 0, 1)
    starts = jnp.swapaxes(start_ref[...], 0, 1)
    ends, gathered = [], []
    for row in range(ROWS):
        source = left(table_ref[...], sources[row])
        eigen = eigen_ref[...] + fine_ref[base + row]
        node_end = source / (1.0 + eigen)
        ends.append(node_end[coarse:])
        source, node_end, eigen = source[:coarse], node_end[:coarse], eigen[:coarse]
        start = starts[row]
        node_mid = 0.5 * (start + source) / (1.0 + 0.5 * eigen)
        rate = source - (1.0 + eigen) * start + (1.0 - eigen) * (4.0 * node_mid + node_end)
        coarse_eigen = coarse_eigen_ref[...] + coarse_ref[base + row]
        gathered.append(factor * (rate / 6.0 + coarse_eigen * node_end))
    out_ref[...] = jnp.swapaxes(jnp.stack(ends), 0, 1)
    gathered_ref[...] = jnp.swapaxes(jnp.stack(gathered), 0, 1)


def offset_kernel(factor, first_ref, coarse_ref, table_ref, coarse_eigen_ref, gathered_ref, start_ref, cubic_ref,
                  out_ref):
    base = pl.program_id(0) * ROWS
    first = first_ref[0] == 1
    cubics = jnp.swapaxes(cubic_ref[...], 0, 1)
    given = jnp.swapaxes(gathered_ref[...] + jnp.where(first, factor * start_ref[...], 0.0), 0, 1)
    rows = []
    for row in range(ROWS):
        total = given[row] - (factor / 6.0) * left(table_ref[...], cubics[row])
        rows.append(total / (1.0 + coarse_eigen_ref[...] + coarse_ref[base + row]))
    out_ref[...] = jnp.swapaxes(jnp.stack(rows), 0, 1)


def finish_kernel(factor, fine_ref, table_ref, eigen_ref, corner_ref, end_ref, *refs):
    out_ref = refs[-1]
    coarse = end_ref.shape[0]
    steps = pl.num_programs(0) // 2
    step = pl.program_id(0)
    base = (step + steps) % (2 * steps) * ROWS
    fields = [joined(refs[n:n + 2]) for n in range(0, 6, 2)]

    def solved(source, eigen):
        source = jnp.swapaxes(source, 0, 1)
        rows = [left(table_ref[...], source[row]) / (1.0 + eigen + fine_ref[base + row]) for row in range(ROWS)]
        return jnp.swapaxes(jnp.stack(rows), 0, 1)

    @pl.when(step < steps)
    def _():
        out_ref[...] = solved(jnp.concatenate(fields[:2], axis=2), eigen_ref[...])

    @pl.when(step >= steps)
    def _():
        out_ref[:coarse, :, :coarse] = end_ref[...] / factor
        out_ref[coarse:, :, :coarse] = corner_ref[...]
        out_ref[:, :, coarse:] = solved(fields[2], eigen_ref[:, coarse:])


def shifted(value, axis, by):
    length = lax.axis_size(axis)
    pairs = [(i, i + by) for i in range(length) if 0 <= i + by < length]
    return lax.ppermute(value, axis, pairs)


def turned(value, axis):
    length = lax.axis_size(axis)
    return lax.ppermute(value, axis, [(i, (i + 1) % length) for i in range(length)])


def exchange(value):
    return lax.all_to_all(value, "gx", split_axis=0, concat_axis=0, tiled=True)


def after(value, *earlier):
    return lax.optimization_barrier((value, *earlier))


def per_device(end_modes, initial_modes):
    grid = initial_modes.shape[0]
    coarse = grid // 2
    groups = lax.axis_size("gx")
    block = grid // groups
    half = block // 2
    planes = 2
    slice_index = lax.axis_index("tm")
    group_index = lax.axis_index("gx")
    is_first = slice_index == 0
    slices = lax.axis_size("tm")
    first = is_first.astype(jnp.int32)[None]
    last = (slice_index == slices - 1).astype(jnp.int32)[None]
    order = fine_order(grid, groups)
    sine = sine_matrix(grid)
    fine_w, coarse_w = omega(grid), omega(coarse)
    factor = ((coarse + 1) / (grid + 1)) ** 1.5
    unit = grid * block * grid

    flat = fine_w[order][:, None] + fine_w[None, :]
    scale = np.array([1.0, 0.5])[:, None, None] * DIFFUSION
    diagonal = 1.0 / scale + 2.0 + flat[None]
    rho = 2.0 / (diagonal + np.sqrt(diagonal * diagonal - 4.0))
    inverse = 1.0 / rho
    kappa = 1.0 / (scale * (inverse - rho))
    rho, inverse, kappa = (t.astype(np.float32) for t in (rho, inverse, kappa))
    rho_slab = (rho.astype(np.float64) ** block).astype(np.float32)
    rounds = 1
    while np.float32(float(rho.max()) ** (block * rounds)) > 0:
        rounds += 1

    depth_table = left_table(sine)
    x_table = right_table(sine)
    y_table = left_table(sine[:, order])
    back_table = left_table(sine[order, :])
    x_low_table = right_table(sine[:, :coarse])
    low_table = left_table(sine[:coarse, :])
    eigen = (DIFFUSION * (fine_w[:, None] + fine_w[None, :])).astype(np.float32)
    coarse_eigen = (0.25 * DIFFUSION * (coarse_w[:, None] + coarse_w[None, :])).astype(np.float32)
    fine_own = lax.dynamic_slice(jnp.asarray((DIFFUSION * fine_w[order]).astype(np.float32)), (group_index * block,), (block,))
    coarse_own = lax.dynamic_slice(
        jnp.asarray((0.25 * DIFFUSION * coarse_w).astype(np.float32)), (group_index * half,), (half,)
    )

    rows_spec = pl.BlockSpec((grid, ROWS, grid), lambda i: (0, i, 0))
    table_spec = whole_block(depth_table.shape)
    shorter = 7 * block // 16 // planes * planes
    lengths = (shorter, block - shorter)
    begins = (0, shorter)
    parts = len(lengths)
    end_begin = begins[1]

    def depth(chosen):
        span = slice(begins[chosen[0]], begins[chosen[-1]] + lengths[chosen[-1]])
        table = depth_table.reshape(groups, block, -1)[:, span].reshape(-1, depth_table.shape[1])
        return pl.pallas_call(
            depth_kernel,
            grid_spec=pltpu.PrefetchScalarGridSpec(
                num_scalar_prefetch=1,
                grid=(block // ROWS,),
                in_specs=[
                    whole_block(table.shape),
                    pl.BlockSpec((grid, ROWS, grid), lambda i, last: (0, i * last[0], 0)),
                    pl.BlockSpec((1, grid, ROWS, grid), lambda i, last: (0, 0, i * (1 - last[0]), 0)),
                ],
                out_specs=[
                    pl.BlockSpec((groups, lengths[part], ROWS, grid), lambda i, last: (0, 0, i, 0))
                    for part in chosen
                ],
            ),
            out_shape=[jax.ShapeDtypeStruct((groups, lengths[part], block, grid), F32) for part in chosen],
            compiler_params=pltpu.CompilerParams(vmem_limit_bytes=VMEM_BYTES),
            cost_estimate=pl.CostEstimate(flops=6 * unit * grid, bytes_accessed=8 * unit, transcendentals=0),
            name="depth",
        )(last, table, initial_modes, end_modes)

    outgoing = [*depth((0,)), *depth((1,))]
    outgoing[0] = turned(outgoing[0], "tm")

    pair = (2, grid, grid)
    pair_spec = whole_block(pair)
    whole = (groups, block, half)
    shapes = [
        (*whole, coarse),
        (groups, block - end_begin, half, grid + coarse),
        (4, block, grid, grid),
    ]
    arrays = None
    state = (np.ones(pair, np.float32), np.zeros(pair, np.float32), np.zeros(pair, np.float32))
    backs, states = {}, {}
    for part in reversed(range(parts)):
        given = outgoing[part]
        if part + 1 in backs:
            given, *_ = after(given, backs[part + 1], *states.get(part + 2, ()))
        backs[part] = exchange(given)
        modes = turned(backs[part], "tm") if part == parts - 1 else backs[part]
        steps = lengths[part] // planes
        bases = [begins[part] // planes] * 3
        if part >= 1:
            bases[1] = (begins[part] - end_begin) // planes
        else:
            shapes[1] = (groups, end_begin, half, grid + coarse)
        specs = [
            pl.BlockSpec(
                (4, planes, grid, grid) if n == 2 else (groups, planes, half, shapes[n][3]),
                lambda i, base=base, steps=steps: (0, base + steps - 1 - i, 0, 0),
            )
            for n, base in enumerate(bases)
        ]
        held = [n for n in range(3) if arrays is not None and not (part == 0 and n == 1)]
        outs = call(
            functools.partial(start_kernel, planes),
            "start",
            (steps,),
            [
                pl.BlockSpec((groups, planes, block, grid), lambda i, steps=steps: (0, steps - 1 - i, 0, 0)),
                whole_block(x_table.shape),
                table_spec,
                table_spec,
                pair_spec,
                pair_spec,
                pair_spec,
                pair_spec,
            ] + [pl.BlockSpec(memory_space=pl.ANY)] * len(held),
            specs + [pair_spec] * 3,
            [jax.ShapeDtypeStruct(shape, F32) for shape in shapes] + [jax.ShapeDtypeStruct(pair, F32)] * 3,
            scratch=[pltpu.VMEM((planes, grid, grid), F32)],
            flops=24 * unit * grid * lengths[part] // block,
            moved=24 * unit * lengths[part] // block,
            aliases={8 + place: n for place, n in enumerate(held)},
        )(modes, x_table, y_table, back_table, rho, *state, *(arrays[n] for n in held))
        if part >= 1:
            rest_last = outs[1]
        else:
            rest_first = outs[1]
        arrays, state = outs[:3], outs[3:]
        states[part] = state
    corner, _, v = arrays
    _, to_right, to_left = state
    rest_last, backs[0] = after(rest_last, backs[0])
    rest_last_back = exchange(rest_last)
    if rounds <= 2 and groups % 2 == 0:
        odd = group_index % 2 == 1
        swap = [(i, i ^ 1) for i in range(groups)]
        partner_right = lax.ppermute(to_right, "gx", swap)
        partner_left = lax.ppermute(to_left, "gx", swap)
        rightward = jnp.where(odd, to_right + rho_slab * partner_right, partner_right + rho_slab * to_right)
        leftward = jnp.where(odd, partner_left + rho_slab * to_left, to_left + rho_slab * partner_left)
        rightward, leftward = after(rightward, leftward)
        before, behind = after(shifted(rightward, "gx", 2), shifted(leftward, "gx", -2))
        before = jnp.where(group_index < 2, -rho * leftward, before)
        behind = jnp.where(group_index >= groups - 2, -rho * rightward, behind)
        from_left = jnp.where(odd, partner_right + rho_slab * before, before)
        from_right = jnp.where(odd, behind, partner_left + rho_slab * behind)
    else:
        at_start, at_end = group_index == 0, group_index == groups - 1
        from_left = jnp.zeros(pair, F32)
        from_right = jnp.zeros(pair, F32)
        for _ in range(rounds):
            rightward = to_right + rho_slab * from_left
            leftward = to_left + rho_slab * from_right
            from_left = jnp.where(at_start, -rho * leftward, shifted(rightward, "gx", 1))
            from_right = jnp.where(at_end, -rho * rightward, shifted(leftward, "gx", -1))

    corner, rest_last_back, from_left, from_right = after(corner, rest_last_back, from_left, from_right)
    corner_back = exchange(corner.reshape(grid, half, coarse))
    node_planes = 2 * planes
    cubic = call(
        functools.partial(node_kernel, node_planes, block),
        "nodes",
        (block // node_planes,),
        [pl.BlockSpec((4, node_planes, grid, grid), lambda i: (0, i, 0, 0))]
        + [pair_spec] * 5
        + [
            whole_block(x_table.shape),
            table_spec,
            whole_block(x_low_table.shape),
            whole_block(low_table.shape),
        ],
        pl.BlockSpec((groups, node_planes, half, coarse), lambda i: (0, i, 0, 0)),
        jax.ShapeDtypeStruct((groups, block, half, coarse), F32),
        scratch=[pltpu.VMEM(pair, F32), pltpu.VMEM(pair, F32), pltpu.VMEM((2, node_planes, grid, grid), F32)],
        flops=28 * unit * grid,
        moved=17 * unit,
    )(v, from_left, from_right, rho, inverse, kappa, x_table, y_table, x_low_table, low_table)
    cubic, corner_back = after(cubic, corner_back)
    cubic_back = exchange(cubic.reshape(grid, half, coarse))
    rest_first, cubic_back = after(rest_first, cubic_back)
    rest_backs = [exchange(rest_first), rest_last_back]
    start_low = jnp.where(
        is_first, initial_modes[:coarse, :half, :coarse], shifted(end_modes[0, :coarse, :half, :coarse], "tm", 1)
    )

    low_spec = pl.BlockSpec((coarse, ROWS, coarse), lambda i: (0, i, 0))
    coarse_eigen_spec = whole_block(coarse_eigen.shape)
    quarter_spec = pl.BlockSpec((grid, ROWS, coarse), lambda i: (0, i, 0))
    corner_shape = jax.ShapeDtypeStruct((coarse, half, coarse), F32)
    result_shape = jax.ShapeDtypeStruct((grid, block, grid), F32)
    corner_end, gathered = call(
        functools.partial(low_kernel, factor),
        "low",
        (half // ROWS,),
        [SMEM, SMEM, table_spec, whole_block((grid, coarse)), coarse_eigen_spec, quarter_spec, low_spec],
        [low_spec, low_spec],
        [corner_shape, corner_shape],
        flops=2 * unit * grid,
        moved=3 * unit,
    )(fine_own, coarse_own, depth_table, eigen[:, :coarse], coarse_eigen, corner_back, start_low)
    offset = call(
        functools.partial(offset_kernel, factor),
        "offset",
        (half // ROWS,),
        [SMEM, SMEM, whole_block(low_table.shape), coarse_eigen_spec, low_spec, low_spec, quarter_spec],
        low_spec,
        corner_shape,
        flops=unit * grid,
        moved=2 * unit,
    )(first, coarse_own, low_table, coarse_eigen, gathered, start_low, cubic_back)

    decay = 1.0 / (1.0 + coarse_eigen[:, None, :] + coarse_own[None, :, None])
    coarse_end = offset
    for turn in range(1, slices):
        incoming = lax.ppermute(coarse_end, "tm", [(turn - 1, turn)])
        coarse_end = jnp.where(slice_index == turn, decay * incoming + offset, coarse_end)
    turns = half // ROWS
    upper = [
        pl.BlockSpec((groups, part.shape[1], ROWS, coarse), lambda i, n=n: (0, 0, jnp.minimum(i, turns - 1), n))
        for n in range(2)
        for part in rest_backs
    ]
    side = [
        pl.BlockSpec((groups, part.shape[1], ROWS, coarse), lambda i: (0, 0, jnp.maximum(i - turns, 0), 2))
        for part in rest_backs
    ]
    corner_spec = pl.BlockSpec((coarse, ROWS, coarse), lambda i: (0, jnp.maximum(i - turns, 0), 0))
    result = call(
        functools.partial(finish_kernel, factor),
        "finish",
        (2 * turns,),
        [SMEM, table_spec, whole_block(eigen.shape), corner_spec, corner_spec] + upper + side,
        pl.BlockSpec((grid, ROWS, grid), lambda i: (0, (i + turns) % (2 * turns), 0)),
        result_shape,
        flops=5 * unit * grid,
        moved=9 * unit,
    )(fine_own, depth_table, eigen, corner_end, coarse_end, *(rest_backs * 3))
    return (result[None], coarse_end[None])


def solution(mesh):
    return jax.shard_map(
        per_device,
        mesh=mesh,
        in_specs=(P("tm", None, "gx", None), P(None, "gx", None)),
        out_specs=(P("tm", None, "gx", None), P("tm", None, "gx", None)),
        check_vma=False,
    )
```
